32 devices in a mesh: dp: 8 (over y, x, core), stream: 4 (over z).
Axes of the slice: x: 2, y: 2, z: 4, core: 2. Of those that a mesh axis runs over, the one named last changes fastest.
Arguments:
- inputs: bfloat16 [32, 1024, 512], P(('dp', 'stream')), may hold values from -60 to 60
- lengths: int32 [32], P(('dp', 'stream')), may hold values from 256 to 1024, as said below
- cotangent: bfloat16 [32, 1024, 512], P(('dp', 'stream')), may hold values from -6 to 6
- gain_one: bfloat16 [512], replicated, may hold values from 0.5 to 1.5
- shift_one: bfloat16 [512], replicated, may hold values from -2.5 to 2.5
- expand_one: bfloat16 [512, 2048], replicated, may hold values from -0.25 to 0.25
- lift_one: bfloat16 [2048], replicated, may hold values from -2.5 to 2.5
- reduce_one: bfloat16 [2048, 512], replicated, may hold values from -0.25 to 0.25
- offset_one: bfloat16 [512], replicated, may hold values from -2.5 to 2.5
- attend_gain: bfloat16 [512], replicated, may hold values from 0.5 to 1.5
- attend_shift: bfloat16 [512], replicated, may hold values from -2.5 to 2.5
- query_proj: bfloat16 [512, 512], replicated, may hold values from -0.25 to 0.25
- query_bias: bfloat16 [512], replicated, may hold values from -2.5 to 2.5
- key_proj: bfloat16 [512, 512], replicated, may hold values from -0.25 to 0.25
- value_proj: bfloat16 [512, 512], replicated, may hold values from -0.25 to 0.25
- value_bias: bfloat16 [512], replicated, may hold values from -2.5 to 2.5
- output_proj: bfloat16 [512, 512], replicated, may hold values from -1 to 1
- output_bias: bfloat16 [512], replicated, may hold values from -2.5 to 2.5
- mixing_gain: bfloat16 [512], replicated, may hold values from 0.5 to 1.5
- mixing_shift: bfloat16 [512], replicated, may hold values from -2.5 to 2.5
- point_first: bfloat16 [512, 1024], replicated, may hold values from -0.25 to 0.25
- first_bias: bfloat16 [1024], replicated, may hold values from -2.5 to 2.5
- depth_kernel: bfloat16 [9, 512], replicated, may hold values from -2 to 2
- batch_gain: bfloat16 [512], replicated, may hold values from 0.5 to 1.5
- batch_shift: bfloat16 [512], replicated, may hold values from -2.5 to 2.5
- point_second: bfloat16 [512, 512], replicated, may hold values from -0.375 to 0.375
- second_bias: bfloat16 [512], replicated, may hold values from -2.5 to 2.5
- gain_two: bfloat16 [512], replicated, may hold values from 0.5 to 1.5
- shift_two: bfloat16 [512], replicated, may hold values from -2.5 to 2.5
- expand_two: bfloat16 [512, 2048], replicated, may hold values from -0.25 to 0.25
- lift_two: bfloat16 [2048], replicated, may hold values from -2.5 to 2.5
- reduce_two: bfloat16 [2048, 512], replicated, may hold values from -0.25 to 0.25
- offset_two: bfloat16 [512], replicated, may hold values from -2.5 to 2.5
- final_gain: bfloat16 [512], replicated, may hold values from 0.5 to 1.5
- final_shift: bfloat16 [512], replicated, may hold values from -2.5 to 2.5
Outputs:
- block_output: bfloat16 [32, 1024, 512], P(('dp', 'stream'))
- input_gradient: bfloat16 [32, 1024, 512], P(('dp', 'stream'))
- gain_one_gradient: float32 [512], replicated
- shift_one_gradient: float32 [512], replicated
- expand_one_gradient: float32 [512, 2048], replicated
- lift_one_gradient: float32 [2048], replicated
- reduce_one_gradient: float32 [2048, 512], replicated
- offset_one_gradient: float32 [512], replicated
- attend_gain_gradient: float32 [512], replicated
- attend_shift_gradient: float32 [512], replicated
- query_proj_gradient: float32 [512, 512], replicated
- query_bias_gradient: float32 [512], replicated
- key_proj_gradient: float32 [512, 512], replicated
- value_proj_gradient: float32 [512, 512], replicated
- value_bias_gradient: float32 [512], replicated
- output_proj_gradient: float32 [512, 512], replicated
- output_bias_gradient: float32 [512], replicated
- mixing_gain_gradient: float32 [512], replicated
- mixing_shift_gradient: float32 [512], replicated
- point_first_gradient: float32 [512, 1024], replicated
- first_bias_gradient: float32 [1024], replicated
- depth_kernel_gradient: float32 [9, 512], replicated
- batch_gain_gradient: float32 [512], replicated
- batch_shift_gradient: float32 [512], replicated
- point_second_gradient: float32 [512, 512], replicated
- second_bias_gradient: float32 [512], replicated
- gain_two_gradient: float32 [512], replicated
- shift_two_gradient: float32 [512], replicated
- expand_two_gradient: float32 [512, 2048], replicated
- lift_two_gradient: float32 [2048], replicated
- reduce_two_gradient: float32 [2048, 512], replicated
- offset_two_gradient: float32 [512], replicated
- final_gain_gradient: float32 [512], replicated
- final_shift_gradient: float32 [512], replicated
- rms_stats: float32 [8], replicated
The draws below stay inside these ranges and needn't reach their ends.
Inputs may be any that keep to these rules, and one draw needn't show every extreme that they name: `lengths`: one utterance has exactly 1024 valid frames and another exactly a quarter of 1024.
All inputs are finite; a program needn't handle non-finite values.
Results may differ from the reference program's by a relative error of at most 0.028.
Values sent between devices are 32-bit elements; how exact they have to be, the bound alone decides.
No kernel may reach another device: no remote copies, remote signals or barrier semaphores. Data moves between devices by JAX's collectives and lax.ppermute only.
A program may use at most 192 MiB of HBM per device.

```python
import math
import jax
import jax.numpy as jnp
from jax import lax

D = 512
HEADS = 8
HEAD = 64
FF = 2048
KERNEL = 9
LEN = 1024
UTTS = 32


def draw_inputs(key, part):
    key = jax.random.fold_in(key, 11)
    noise_key, offset_key, factor_key = jax.random.split(key, 3)
    position = jnp.arange(UTTS, dtype=jnp.float32) / max(UTTS - 1, 1)
    noise_part = jax.random.truncated_normal(noise_key, -4.0, 4.0, (UTTS, LEN, D), jnp.float32)
    rising = jnp.exp(position * math.log(3.0))
    lean_weight = 0.8
    offsets = jax.random.truncated_normal(offset_key, -3.0, 3.0, (UTTS, 1, D), jnp.float32)
    factor = jax.random.uniform(factor_key, (UTTS, 1, 1), jnp.float32, 0.75, 1.25)
    return (rising[:, None, None] * factor * (noise_part + lean_weight * offsets)).astype(jnp.bfloat16)


def draw_lengths(key, part):
    key = jax.random.fold_in(key, 23)
    base_key, first_key, second_key = jax.random.split(key, 3)
    drawn = jax.random.randint(base_key, (UTTS,), LEN // 4, LEN + 1)
    longest = jax.random.randint(first_key, (), 0, UTTS)
    shortest = (longest + jax.random.randint(second_key, (), 1, UTTS)) % UTTS
    slot_index = jnp.arange(UTTS, dtype=jnp.int32)
    drawn = jnp.where(slot_index == longest, LEN, drawn)
    drawn = jnp.where(slot_index == shortest, LEN // 4, drawn)
    return drawn.astype(jnp.int32)


def block_scale(rng, extent, cuts, low, largest):
    level, own = 1.0, jax.random.fold_in(rng, 6)
    for axis_at, blocks in cuts:
        steps = jnp.exp(jax.random.uniform(jax.random.fold_in(own, axis_at), (blocks,), jnp.float32, low / len(cuts), largest / len(cuts)))
        level = level * jnp.repeat(steps, extent[axis_at] // blocks).reshape([-1 if axis == axis_at else 1 for axis in range(len(extent))])
    return level


def noise(rng, extent, deviation, most, cuts=(), held_as=jnp.bfloat16):
    array = jax.random.normal(rng, extent, jnp.float32) * deviation
    if len(cuts) > 0:
        array = block_scale(rng, extent, cuts, -0.22, 0.18) * array
    return jnp.clip(array, min=-most, max=most).astype(held_as)


def setup_inputs(seed: int = 0) -> dict:
    key_list = jax.random.split(jax.random.key(seed), 36)
    inputs = draw_inputs(jax.random.fold_in(key_list[35], 71), 0)
    lengths = draw_lengths(jax.random.fold_in(key_list[35], 71), 0)
    cotangent = noise(key_list[2], (UTTS, LEN, D), 1.0, 6.0, ((0, 32),))
    gain_one = jnp.clip(1.0 + 0.1 * jax.random.normal(key_list[3], (D,), jnp.float32), 0.5, 1.5).astype(jnp.bfloat16)
    shift_one = noise(key_list[4], (D,), 0.3, 2.5)
    expand_one = noise(key_list[5], (D, FF), D ** -0.5, 0.25)
    lift_one = noise(key_list[6], (FF,), 0.3, 2.5)
    reduce_one = noise(key_list[7], (FF, D), (FF // 4) ** -0.5, 0.25)
    offset_one = noise(key_list[8], (D,), 0.3, 2.5)
    attend_gain = jnp.clip(1.0 + 0.1 * jax.random.normal(key_list[9], (D,), jnp.float32), 0.5, 1.5).astype(jnp.bfloat16)
    attend_shift = noise(key_list[10], (D,), 0.3, 2.5)
    query_proj = noise(key_list[11], (D, D), D ** -0.5, 0.25)
    query_bias = noise(key_list[12], (D,), 0.3, 2.5)
    key_proj = noise(key_list[13], (D, D), D ** -0.5, 0.25)
    value_proj = noise(key_list[14], (D, D), D ** -0.5, 0.25)
    value_bias = noise(key_list[15], (D,), 0.3, 2.5)
    output_proj = noise(key_list[16], (D, D), (D // 16) ** -0.5, 1.0)
    output_bias = noise(key_list[17], (D,), 0.3, 2.5)
    mixing_gain = jnp.clip(1.0 + 0.1 * jax.random.normal(key_list[18], (D,), jnp.float32), 0.5, 1.5).astype(jnp.bfloat16)
    mixing_shift = noise(key_list[19], (D,), 0.3, 2.5)
    point_first = noise(key_list[20], (D, 2 * D), D ** -0.5, 0.25)
    first_bias = noise(key_list[21], (2 * D,), 0.3, 2.5)
    depth_kernel = noise(key_list[22], (KERNEL, D), KERNEL ** -0.5, 2.0)
    batch_gain = jnp.clip(1.0 + 0.1 * jax.random.normal(key_list[23], (D,), jnp.float32), 0.5, 1.5).astype(jnp.bfloat16)
    batch_shift = noise(key_list[24], (D,), 0.3, 2.5)
    point_second = noise(key_list[25], (D, D), (D // 2) ** -0.5, 0.375)
    second_bias = noise(key_list[26], (D,), 0.3, 2.5)
    gain_two = jnp.clip(1.0 + 0.1 * jax.random.normal(key_list[27], (D,), jnp.float32), 0.5, 1.5).astype(jnp.bfloat16)
    shift_two = noise(key_list[28], (D,), 0.3, 2.5)
    expand_two = noise(key_list[29], (D, FF), D ** -0.5, 0.25)
    lift_two = noise(key_list[30], (FF,), 0.3, 2.5)
    reduce_two = noise(key_list[31], (FF, D), (FF // 4) ** -0.5, 0.25)
    offset_two = noise(key_list[32], (D,), 0.3, 2.5)
    final_gain = jnp.clip(1.0 + 0.1 * jax.random.normal(key_list[33], (D,), jnp.float32), 0.5, 1.5).astype(jnp.bfloat16)
    final_shift = noise(key_list[34], (D,), 0.3, 2.5)
    return dict(inputs=inputs, lengths=lengths, cotangent=cotangent, gain_one=gain_one, shift_one=shift_one, expand_one=expand_one, lift_one=lift_one, reduce_one=reduce_one, offset_one=offset_one, attend_gain=attend_gain, attend_shift=attend_shift, query_proj=query_proj, query_bias=query_bias, key_proj=key_proj, value_proj=value_proj, value_bias=value_bias, output_proj=output_proj, output_bias=output_bias, mixing_gain=mixing_gain, mixing_shift=mixing_shift, point_first=point_first, first_bias=first_bias, depth_kernel=depth_kernel, batch_gain=batch_gain, batch_shift=batch_shift, point_second=point_second, second_bias=second_bias, gain_two=gain_two, shift_two=shift_two, expand_two=expand_two, lift_two=lift_two, reduce_two=reduce_two, offset_two=offset_two, final_gain=final_gain, final_shift=final_shift)


@jax.custom_vjp
def low(v):
    return lax.optimization_barrier(v.astype(jnp.bfloat16)).astype(jnp.float32)

@jax.custom_vjp
def low_back(v):
    return v

def low_keep(v):
    return (low(v), None)

def low_pass(kept, grad):
    return (grad,)

def back_keep(v):
    return (v, None)

def back_low(kept, grad):
    return (low(grad),)
low.defvjp(low_keep, low_pass)
low_back.defvjp(back_keep, back_low)
EPSILON = 1e-05

def matmul(operand_one, operand_two):
    return jnp.dot(operand_one, operand_two, precision=lax.Precision.HIGHEST, preferred_element_type=jnp.float32)

def layer_norm(values, norm_gain, norm_shift):
    centre = lax.optimization_barrier(jnp.mean(values, axis=-1, keepdims=True))
    centred = values - centre
    spread = lax.optimization_barrier(jnp.mean(centred * centred, axis=-1, keepdims=True))
    return centred * lax.rsqrt(spread + EPSILON) * norm_gain + norm_shift

def depthwise(shaped, kernel):
    half_width = kernel.shape[0] // 2
    frames = shaped.shape[1]
    padded = jnp.pad(shaped, ((0, 0), (half_width, half_width), (0, 0)))
    summed = padded[:, 0:frames, :] * kernel[0]
    for tap_index in range(1, kernel.shape[0]):
        summed = summed + padded[:, tap_index:tap_index + frames, :] * kernel[tap_index]
    return summed

def gate_convolve(both_halves, kernel, validity_rows, utterances):
    half_cols = both_halves.shape[1] // 2
    gated_rows = both_halves[:, :half_cols] * jax.nn.sigmoid(both_halves[:, half_cols:]) * validity_rows
    shaped = gated_rows.reshape(utterances, -1, half_cols)
    return depthwise(shaped, kernel).reshape(-1, half_cols)

def feed_forward(row_data, params):
    norm_gain, norm_shift, expand, lift_bias, reducer, offset = params
    normed = low(layer_norm(row_data, norm_gain, norm_shift))
    inner_act = low_back(matmul(normed, expand) + lift_bias)
    activated = low(jax.nn.silu(inner_act))
    return 0.5 * low_back(matmul(activated, reducer) + offset)

def attention(row_data, mask_group, params):
    norm_gain, norm_shift, query_proj, query_bias, key_proj, value_proj, value_bias, output_proj, output_bias = params
    layout = (mask_group.shape[0], LEN, HEADS, HEAD)
    normed = low(layer_norm(row_data, norm_gain, norm_shift))
    queries = low(low_back(matmul(normed, query_proj) + query_bias)).reshape(layout)
    key_rows = low(low_back(matmul(normed, key_proj))).reshape(layout)
    value_rows = low(low_back(matmul(normed, value_proj) + value_bias)).reshape(layout)
    scores = low_back(jnp.einsum('bqhd,bkhd->bhqk', queries, key_rows, precision=lax.Precision.HIGHEST) * HEAD ** (-0.5))
    scores = jnp.where(mask_group[:, None, None, :] > 0.5, scores, -1e+30)
    softened = low(jax.nn.softmax(scores, axis=-1))
    mixture = low(low_back(jnp.einsum('bhqk,bkhd->bqhd', softened, value_rows, precision=lax.Precision.HIGHEST)))
    return low_back(matmul(mixture.reshape(-1, D), output_proj) + output_bias)

def mixing_front(row_data, params, validity_rows, utterances):
    norm_gain, norm_shift, point_first, first_bias, depth_kernel = params
    normed = low(layer_norm(row_data, norm_gain, norm_shift))
    doubled = low_back(matmul(normed, point_first) + first_bias)
    return gate_convolve(doubled, depth_kernel, validity_rows, utterances)

def mixing_rear(convolved, batch_mean, batch_var, params):
    batch_gain, batch_shift, point_second, second_bias = params
    normal_out = (convolved - batch_mean) * lax.rsqrt(batch_var + EPSILON) * batch_gain + batch_shift
    activated = low(jax.nn.silu(normal_out))
    return low_back(matmul(activated, point_second) + second_bias)

def masked_square(section, validity_rows):
    return jnp.sum(validity_rows * section * section)

def reference(inputs, lengths, cotangent, gain_one, shift_one, expand_one, lift_one, reduce_one, offset_one, attend_gain, attend_shift, query_proj, query_bias, key_proj, value_proj, value_bias, output_proj, output_bias, mixing_gain, mixing_shift, point_first, first_bias, depth_kernel, batch_gain, batch_shift, point_second, second_bias, gain_two, shift_two, expand_two, lift_two, reduce_two, offset_two, final_gain, final_shift):
    weights = [argument.astype(jnp.float32) for argument in (gain_one, shift_one, expand_one, lift_one, reduce_one, offset_one, attend_gain, attend_shift, query_proj, query_bias, key_proj, value_proj, value_bias, output_proj, output_bias, mixing_gain, mixing_shift, point_first, first_bias, depth_kernel, batch_gain, batch_shift, point_second, second_bias, gain_two, shift_two, expand_two, lift_two, reduce_two, offset_two, final_gain, final_shift)]
    group_size = math.gcd(UTTS, max(1, 4096 // LEN))
    group_count = UTTS // group_size
    validity = (jnp.arange(LEN, dtype=jnp.int32)[None, :] < lengths[:, None]).astype(jnp.float32)
    validity_groups = validity.reshape(group_count, group_size, LEN)
    frame_count = jnp.sum(validity)

    def forward(stream, *params):
        first_block = params[0:6]
        attend_block = params[6:15]
        mixing_block = params[15:24]
        second_block = params[24:30]
        closing_gain = params[30]
        closing_shift = params[31]

        def front_part(pieces):
            stream_group, mask_group = pieces
            validity_rows = mask_group.reshape(-1, 1)
            row_data = stream_group.reshape(-1, D)
            first_branch = feed_forward(row_data, first_block)
            after_first = row_data + first_branch
            attend_branch = attention(after_first, mask_group, attend_block)
            after_attend = after_first + attend_branch
            convolved = mixing_front(after_attend, mixing_block[0:5], validity_rows, group_size)
            squares = jnp.stack([masked_square(section, validity_rows) for section in (after_first, after_attend, first_branch, attend_branch)])
            return (after_attend, convolved, squares)
        attended, convolved, front_squares = lax.map(jax.checkpoint(front_part), (stream.reshape(group_count, group_size, LEN, D), validity_groups))
        mask_column = validity_groups.reshape(group_count, group_size * LEN, 1)
        batch_mean = lax.optimization_barrier(jnp.sum(convolved * mask_column, axis=(0, 1))) / frame_count
        centred = (convolved - batch_mean) * mask_column
        batch_var = lax.optimization_barrier(jnp.sum(centred * centred, axis=(0, 1))) / frame_count

        def rear_part(pieces):
            after_attend, convolved_group, mask_group = pieces
            validity_rows = mask_group.reshape(-1, 1)
            mixing_branch = mixing_rear(convolved_group, batch_mean, batch_var, mixing_block[5:9])
            after_mixing = after_attend + mixing_branch
            second_branch = feed_forward(after_mixing, second_block)
            after_second = after_mixing + second_branch
            output = validity_rows * layer_norm(after_second, closing_gain, closing_shift)
            squares = jnp.stack([masked_square(section, validity_rows) for section in (after_mixing, after_second, mixing_branch, second_branch)])
            return (output, squares)
        output, rear_squares = lax.map(jax.checkpoint(rear_part), (attended, convolved, validity_groups))
        front_total = lax.optimization_barrier(jnp.sum(front_squares, axis=0))
        rear_total = lax.optimization_barrier(jnp.sum(rear_squares, axis=0))
        totals = jnp.concatenate([front_total[0:2], rear_total[0:2], front_total[2:4], rear_total[2:4]])
        return (output.reshape(UTTS, LEN, D), jnp.sqrt(totals / (frame_count * D)))
    result, pullback, rms_values = jax.vjp(forward, inputs.astype(jnp.float32), *weights, has_aux=True)
    gradients = pullback(cotangent.astype(jnp.float32))
    return (result.astype(jnp.bfloat16), gradients[0].astype(jnp.bfloat16), *gradients[1:], rms_values)
```

```python
import jax
import jax.numpy as jnp
from jax import lax
from jax.sharding import PartitionSpec as P

HEADS = 8
HEAD = 64


EPSILON = 1e-05


def product(operand_one, operand_two):
    return jnp.dot(operand_one, operand_two, preferred_element_type=jnp.float32)


def row_contract(operand_one, operand_two):
    return lax.dot_general(
        operand_one, operand_two, (((0,), (0,)), ((), ())), preferred_element_type=jnp.float32
    )


def transposed_product(operand_one, operand_two):
    return lax.dot_general(
        operand_one, operand_two, (((1,), (1,)), ((), ())), preferred_element_type=jnp.float32
    )


def column_sum(values):
    return jnp.sum(values, axis=0, dtype=jnp.float32)


AXES = ("dp", "stream")


def bits_of(axis):
    return lax.axis_size(axis).bit_length() - 1


def exchange(values, axis, bit):
    count = lax.axis_size(axis)
    return lax.ppermute(values, axis, [(at, at ^ (1 << bit)) for at in range(count)])


def own_bit(axis, bit):
    return (lax.axis_index(axis) >> bit) & 1


def every_bit():
    return [(axis, bit) for axis in AXES for bit in range(bits_of(axis))]


def halve(values, axis, bit):
    half = values.shape[0] // 2
    mine = own_bit(axis, bit)
    arrived = exchange(
        lax.dynamic_slice_in_dim(values, (1 - mine) * half, half), axis, bit
    )
    return lax.dynamic_slice_in_dim(values, mine * half, half) + arrived


def double(values, axis, bit):
    arrived = exchange(values, axis, bit)
    upper = own_bit(axis, bit) == 1
    return jnp.concatenate(
        [jnp.where(upper, arrived, values), jnp.where(upper, values, arrived)]
    )


def sum_parts(parts):
    pair = every_bit()[0]
    rest_dp = [step for step in every_bit()[1:] if step[0] == "dp"]
    rest_stream = [step for step in every_bit() if step[0] == "stream"]
    orders = [
        [pair] + rest_dp + rest_stream,
        [pair] + rest_dp[::-1] + rest_stream,
        [pair] + rest_stream + rest_dp,
    ]
    steps = len(orders[0])
    for at in range(steps):
        parts = [halve(part, *orders[which % 3][at]) for which, part in enumerate(parts)]
    for at in reversed(range(steps)):
        parts = [double(part, *orders[which % 3][at]) for which, part in enumerate(parts)]
    return parts


def sum_small(values):
    for axis, bit in every_bit():
        values = values + exchange(values, axis, bit)
    return values


def batch_moments(convolved, validity_rows):
    count = jnp.sum(validity_rows)
    summed = column_sum(convolved * validity_rows)
    apart = (convolved - summed / count) * validity_rows
    spread = column_sum(apart * apart)
    packed = jnp.stack([jnp.full_like(summed, count), summed, spread])
    for axis, bit in every_bit():
        other = exchange(packed, axis, bit)
        both = packed + other
        gap = packed[1] / packed[0] - other[1] / other[0]
        extra = gap * gap * (packed[0] * other[0] / both[0])
        packed = jnp.stack([both[0], both[1], both[2] + extra])
    return packed[0, 0], packed[1] / packed[0], packed[2] / packed[0]


def layer_norm(values, norm_gain, norm_shift):
    centre = jnp.mean(values, axis=-1, keepdims=True)
    centred = values - centre
    spread = jnp.mean(centred * centred, axis=-1, keepdims=True)
    return centred * lax.rsqrt(spread + EPSILON) * norm_gain + norm_shift


def silu_slope(inner_act):
    logistic = jax.nn.sigmoid(inner_act)
    return logistic * (1.0 + inner_act * (1.0 - logistic))


def depthwise(shaped, kernel):
    half_width = kernel.shape[0] // 2
    frames = shaped.shape[1]
    padded = jnp.pad(shaped, ((0, 0), (half_width, half_width), (0, 0)))
    summed = padded[:, 0:frames, :] * kernel[0]
    for tap_index in range(1, kernel.shape[0]):
        summed = summed + padded[:, tap_index : tap_index + frames, :] * kernel[tap_index]
    return summed


def gate_convolve(both_halves, kernel, validity_rows, utterances):
    half_cols = both_halves.shape[1] // 2
    gated_rows = (
        both_halves[:, :half_cols] * jax.nn.sigmoid(both_halves[:, half_cols:]) * validity_rows
    )
    shaped = gated_rows.reshape(utterances, -1, half_cols)
    return depthwise(shaped, kernel).reshape(-1, half_cols)


def norm_forward(stream, norm_gain, norm_shift):
    return jax.vjp(
        layer_norm, stream, norm_gain.astype(jnp.float32), norm_shift.astype(jnp.float32)
    )


def feed_forward(stream, params):
    norm_gain, norm_shift, expand, lift_bias, reducer, offset = params
    normed, norm_back = norm_forward(stream, norm_gain, norm_shift)
    normed_low = normed.astype(jnp.bfloat16)
    inner_act = product(normed_low, expand) + lift_bias.astype(jnp.float32)
    activated = jax.nn.silu(inner_act).astype(jnp.bfloat16)
    branch = 0.5 * (product(activated, reducer) + offset.astype(jnp.float32))
    return (branch, (norm_back, normed_low, inner_act, activated))


def feed_backward(grad_stream, params, stored):
    norm_gain, norm_shift, expand, lift_bias, reducer, offset = params
    norm_back, normed_low, inner_act, activated = stored
    branch_low = (0.5 * grad_stream).astype(jnp.bfloat16)
    grad_reducer = row_contract(activated, branch_low)
    grad_offset = column_sum(branch_low)
    grad_activated = transposed_product(branch_low, reducer)
    inner_low = (grad_activated * silu_slope(inner_act)).astype(jnp.bfloat16)
    grad_expand = row_contract(normed_low, inner_low)
    grad_lift = column_sum(inner_low)
    grad_input, grad_gain, grad_shift = norm_back(transposed_product(inner_low, expand))
    return (
        grad_stream + grad_input,
        [grad_gain, grad_shift, grad_expand, grad_lift, grad_reducer, grad_offset],
    )


def masked_scores(query_block, keys_here, mask_here):
    scores = jnp.einsum(
        "qhd,khd->hqk", query_block, keys_here, preferred_element_type=jnp.float32
    ) * HEAD ** (-0.5)
    return jnp.where(mask_here[None, None, :], scores, -1e30)


def attend_forward(stream, params, key_mask):
    (
        norm_gain,
        norm_shift,
        query_proj,
        query_bias,
        key_proj,
        value_proj,
        value_bias,
        output_proj,
        output_bias,
    ) = params
    utterances, frames = key_mask.shape
    normed, norm_back = norm_forward(stream, norm_gain, norm_shift)
    normed_low = normed.astype(jnp.bfloat16)
    layout = (utterances, frames, HEADS, HEAD)
    queries = (
        (product(normed_low, query_proj) + query_bias.astype(jnp.float32))
        .astype(jnp.bfloat16)
        .reshape(layout)
    )
    key_rows = product(normed_low, key_proj).astype(jnp.bfloat16).reshape(layout)
    value_rows = (
        (product(normed_low, value_proj) + value_bias.astype(jnp.float32))
        .astype(jnp.bfloat16)
        .reshape(layout)
    )
    block_rows = min(512, frames)
    block_count = frames // block_rows
    keys_here = key_rows[0]
    values_here = value_rows[0]
    mask_here = key_mask[0]

    def forward_block(carried, query_block):
        scores = masked_scores(query_block, keys_here, mask_here)
        row_top = jnp.max(scores, axis=-1, keepdims=True)
        raised = jnp.exp(scores - row_top)
        totals = jnp.sum(raised, axis=-1, keepdims=True)
        softened = (raised / totals).astype(jnp.bfloat16)
        mixture = jnp.einsum(
            "hqk,khd->qhd", softened, values_here, preferred_element_type=jnp.float32
        )
        return (carried, (mixture.astype(jnp.bfloat16), row_top + jnp.log(totals)))

    unused, (mixture, log_total) = lax.scan(
        forward_block, 0, queries[0].reshape(block_count, block_rows, HEADS, HEAD)
    )
    mixtures = mixture.reshape(frames, HEADS * HEAD)
    log_totals = [log_total]
    branch = product(mixtures, output_proj) + output_bias.astype(jnp.float32)
    return (branch, (norm_back, normed_low, queries, key_rows, value_rows, mixtures, log_totals))


def attend_backward(grad_stream, params, stored, key_mask):
    (
        norm_gain,
        norm_shift,
        query_proj,
        query_bias,
        key_proj,
        value_proj,
        value_bias,
        output_proj,
        output_bias,
    ) = params
    norm_back, normed_low, queries, key_rows, value_rows, mixed, log_totals = stored
    utterances, frames = key_mask.shape
    block_rows = min(512, frames)
    block_count = frames // block_rows
    out_low = grad_stream.astype(jnp.bfloat16)
    grad_output = row_contract(mixed, out_low)
    grad_output_bias = column_sum(out_low)
    grad_mixed = (
        transposed_product(out_low, output_proj)
        .astype(jnp.bfloat16)
        .reshape(utterances, frames, HEADS, HEAD)
    )
    keys_here = key_rows[0]
    values_here = value_rows[0]
    mask_here = key_mask[0]

    def backward_block(carried, pieces):
        keys_total, values_total = carried
        query_block, mixed_block, log_block = pieces
        softened = jnp.exp(masked_scores(query_block, keys_here, mask_here) - log_block)
        soft_low = softened.astype(jnp.bfloat16)
        values_total = values_total + jnp.einsum(
            "hqk,qhd->khd", soft_low, mixed_block, preferred_element_type=jnp.float32
        )
        grad_soft = jnp.einsum(
            "qhd,khd->hqk", mixed_block, values_here, preferred_element_type=jnp.float32
        )
        inner_sum = jnp.sum(softened * grad_soft, axis=-1, keepdims=True)
        score_low = (softened * (grad_soft - inner_sum)).astype(jnp.bfloat16)
        query_grad = (
            jnp.einsum("hqk,khd->qhd", score_low, keys_here, preferred_element_type=jnp.float32)
            * HEAD ** (-0.5)
        ).astype(jnp.bfloat16)
        keys_total = keys_total + jnp.einsum(
            "hqk,qhd->khd", score_low, query_block, preferred_element_type=jnp.float32
        ) * HEAD ** (-0.5)
        return ((keys_total, values_total), query_grad)

    zeros_here = jnp.zeros((frames, HEADS, HEAD), jnp.float32)
    (keys_total, values_total), query_grad = lax.scan(
        backward_block,
        (zeros_here, zeros_here),
        (
            queries[0].reshape(block_count, block_rows, HEADS, HEAD),
            grad_mixed[0].reshape(block_count, block_rows, HEADS, HEAD),
            log_totals[0],
        ),
    )
    query_grads = query_grad.reshape(frames, HEADS * HEAD)
    key_grads = keys_total.astype(jnp.bfloat16).reshape(frames, HEADS * HEAD)
    value_grads = values_total.astype(jnp.bfloat16).reshape(frames, HEADS * HEAD)
    grad_normed = transposed_product(query_grads, query_proj) + transposed_product(
        key_grads, key_proj
    )
    grad_normed = grad_normed + transposed_product(value_grads, value_proj)
    grad_input, grad_gain, grad_shift = norm_back(grad_normed)
    return (
        grad_stream + grad_input,
        [
            grad_gain,
            grad_shift,
            row_contract(normed_low, query_grads),
            column_sum(query_grads),
            row_contract(normed_low, key_grads),
            row_contract(normed_low, value_grads),
            column_sum(value_grads),
            grad_output,
            grad_output_bias,
        ],
    )


def mixing_front(stream, params, validity_rows, utterances):
    norm_gain, norm_shift, point_first, first_bias, depth_kernel = params[0:5]
    normed, norm_back = norm_forward(stream, norm_gain, norm_shift)
    normed_low = normed.astype(jnp.bfloat16)
    doubled = product(normed_low, point_first) + first_bias.astype(jnp.float32)
    convolved, front_back = jax.vjp(
        lambda both_halves, kernel: gate_convolve(both_halves, kernel, validity_rows, utterances),
        doubled,
        depth_kernel.astype(jnp.float32),
    )
    return (convolved, (norm_back, normed_low, front_back))


def mixing_rear(convolved, batch_mean, inverse_std, params):
    batch_gain, batch_shift, point_second, second_bias = params[5:9]
    centred = convolved - batch_mean
    normal_out = centred * inverse_std * batch_gain.astype(jnp.float32) + batch_shift.astype(
        jnp.float32
    )
    activated = jax.nn.silu(normal_out).astype(jnp.bfloat16)
    branch = product(activated, point_second) + second_bias.astype(jnp.float32)
    return (branch, (centred, normal_out, activated))


def mixing_backward(
    grad_stream, params, front_stored, rear_stored, validity_rows, frame_count, inverse_std
):
    point_first = params[2]
    batch_gain = params[5]
    point_second = params[7]
    norm_back, normed_low, front_back = front_stored
    centred, normal_out, activated = rear_stored
    low_grad = grad_stream.astype(jnp.bfloat16)
    grad_point_second = row_contract(activated, low_grad)
    grad_second_bias = column_sum(low_grad)
    grad_normal = transposed_product(low_grad, point_second) * silu_slope(normal_out)
    grad_batch_gain = column_sum(grad_normal * centred * inverse_std)
    grad_batch_shift = column_sum(grad_normal)
    direct = grad_normal * batch_gain.astype(jnp.float32) * inverse_std
    mean_total, spread_total = sum_small(
        jnp.stack(
            [-column_sum(direct), -0.5 * inverse_std * inverse_std * column_sum(direct * centred)]
        )
    )
    grad_convolved = (
        direct + validity_rows * (mean_total + 2.0 * spread_total * centred) / frame_count
    )
    grad_doubled, grad_kernel = front_back(grad_convolved)
    doubled_low = grad_doubled.astype(jnp.bfloat16)
    grad_point_first = row_contract(normed_low, doubled_low)
    grad_first_bias = column_sum(doubled_low)
    grad_input, grad_gain, grad_shift = norm_back(transposed_product(doubled_low, point_first))
    return (
        grad_stream + grad_input,
        [
            grad_gain,
            grad_shift,
            grad_point_first,
            grad_first_bias,
            grad_kernel,
            grad_batch_gain,
            grad_batch_shift,
            grad_point_second,
            grad_second_bias,
        ],
    )


def body(
    inputs,
    lengths,
    cotangent,
    gain_one,
    shift_one,
    expand_one,
    lift_one,
    reduce_one,
    offset_one,
    attend_gain,
    attend_shift,
    query_proj,
    query_bias,
    key_proj,
    value_proj,
    value_bias,
    output_proj,
    output_bias,
    mixing_gain,
    mixing_shift,
    point_first,
    first_bias,
    depth_kernel,
    batch_gain,
    batch_shift,
    point_second,
    second_bias,
    gain_two,
    shift_two,
    expand_two,
    lift_two,
    reduce_two,
    offset_two,
    final_gain,
    final_shift,
):
    first_block = [gain_one, shift_one, expand_one, lift_one, reduce_one, offset_one]
    attend_block = [
        attend_gain,
        attend_shift,
        query_proj,
        query_bias,
        key_proj,
        value_proj,
        value_bias,
        output_proj,
        output_bias,
    ]
    mixing_block = [
        mixing_gain,
        mixing_shift,
        point_first,
        first_bias,
        depth_kernel,
        batch_gain,
        batch_shift,
        point_second,
        second_bias,
    ]
    second_block = [gain_two, shift_two, expand_two, lift_two, reduce_two, offset_two]
    utterances, frames, model_width = inputs.shape
    key_mask = lax.broadcasted_iota(jnp.int32, (utterances, frames), 1) < lengths[:, None]
    validity_rows = key_mask.astype(jnp.float32).reshape(utterances * frames, 1)
    stream = inputs.astype(jnp.float32).reshape(-1, model_width)
    first_branch, first_stored = feed_forward(stream, first_block)
    after_first = stream + first_branch
    attend_branch, attend_stored = attend_forward(after_first, attend_block, key_mask)
    after_attend = after_first + attend_branch
    convolved, front_stored = mixing_front(after_attend, mixing_block, validity_rows, utterances)
    frame_count, batch_mean, batch_var = batch_moments(convolved, validity_rows)
    inverse_std = lax.rsqrt(batch_var + EPSILON)
    mixing_branch, rear_stored = mixing_rear(convolved, batch_mean, inverse_std, mixing_block)
    after_mixing = after_attend + mixing_branch
    second_branch, second_stored = feed_forward(after_mixing, second_block)
    after_second = after_mixing + second_branch
    output, final_back = jax.vjp(
        lambda section, norm_gain, norm_shift: validity_rows
        * layer_norm(section, norm_gain, norm_shift),
        after_second,
        final_gain.astype(jnp.float32),
        final_shift.astype(jnp.float32),
    )
    squares = jnp.stack(
        [
            jnp.sum(validity_rows * section * section)
            for section in (
                after_first,
                after_attend,
                after_mixing,
                after_second,
                first_branch,
                attend_branch,
                mixing_branch,
                second_branch,
            )
        ]
    )
    grad_after, closing_gain, closing_shift = final_back(
        cotangent.astype(jnp.float32).reshape(-1, model_width)
    )
    grad_after, second_grads = feed_backward(grad_after, second_block, second_stored)
    second_large = lax.psum((second_grads[2], second_grads[4]), AXES)
    grad_after, mixing_grads = mixing_backward(
        grad_after, mixing_block, front_stored, rear_stored, validity_rows, frame_count, inverse_std
    )
    grad_after, attend_grads = attend_backward(grad_after, attend_block, attend_stored, key_mask)
    width = model_width
    rows = []
    for piece in (
        second_grads[0],
        second_grads[1],
        second_grads[3],
        second_grads[5],
        *mixing_grads[0:2],
        *mixing_grads[3:7],
        mixing_grads[8],
        closing_gain,
        closing_shift,
        *attend_grads[0:2],
        attend_grads[3],
        attend_grads[6],
        attend_grads[8],
        jnp.pad(squares, (0, width - 8)),
    ):
        rows.append(piece.reshape(-1, width))
    small = jnp.concatenate(rows)
    small_rows = small.shape[0]
    small = jnp.pad(small, ((0, 128 - small_rows), (0, 0)))
    large = jnp.concatenate(
        [
            mixing_grads[2][:, :width],
            mixing_grads[2][:, width:],
            mixing_grads[7],
            attend_grads[2],
            attend_grads[4],
            attend_grads[5],
            attend_grads[7],
            small,
        ]
    )
    cut = 1408
    middle = jnp.concatenate(sum_parts([large[:cut], large[cut : 2 * cut], large[2 * cut :]]))
    grad_after, first_grads = feed_backward(grad_after, first_block, first_stored)
    first_reduce, first_expand = sum_parts([first_grads[4], first_grads[2]])
    first_small = sum_small(
        jnp.concatenate(
            [
                first_grads[0][None],
                first_grads[1][None],
                first_grads[3].reshape(-1, width),
                first_grads[5][None],
            ]
        )
    )
    squares = middle[7 * width + small_rows - 1, 0:8]
    at = [7 * width]

    def take(count):
        piece = middle[at[0] : at[0] + count].reshape(-1)
        at[0] = at[0] + count
        return piece

    second_sums = [take(1), take(1), second_large[0], take(4), second_large[1], take(1)]
    mixing_sums = [take(1), take(1), None, take(2)]
    mixing_sums = mixing_sums + [
        middle[at[0] : at[0] + 9],
    ]
    at[0] = at[0] + 9
    mixing_sums = mixing_sums + [take(1), take(1), middle[2 * width : 3 * width], take(1)]
    mixing_sums[2] = jnp.concatenate([middle[:width], middle[width : 2 * width]], axis=1)
    closing_sums = [take(1), take(1)]
    attend_sums = [take(1), take(1), None, take(1), None, None, take(1), None, take(1)]
    for slot, block in ((2, 3), (4, 4), (5, 5), (7, 6)):
        attend_sums[slot] = middle[block * width : (block + 1) * width]
    first_sums = [
        first_small[0],
        first_small[1],
        first_expand,
        first_small[2:-1].reshape(-1),
        first_reduce,
        first_small[-1],
    ]
    rms_stats = jnp.sqrt(squares / (frame_count * model_width))
    block_output = output.reshape(utterances, frames, model_width).astype(jnp.bfloat16)
    input_gradient = grad_after.reshape(utterances, frames, model_width).astype(jnp.bfloat16)
    return (
        block_output,
        input_gradient,
        *first_sums,
        *attend_sums,
        *mixing_sums,
        *second_sums,
        *closing_sums,
        rms_stats,
    )


def solution(mesh):
    placed = (
        P(("dp", "stream"), None, None),
        P(("dp", "stream")),
        P(("dp", "stream"), None, None),
        P(),
        P(),
        P(),
        P(),
        P(),
        P(),
        P(),
        P(),
        P(),
        P(),
        P(),
        P(),
        P(),
        P(),
        P(),
        P(),
        P(),
        P(),
        P(),
        P(),
        P(),
        P(),
        P(),
        P(),
        P(),
        P(),
        P(),
        P(),
        P(),
        P(),
        P(),
        P(),
    )
    return jax.shard_map(
        body,
        mesh=mesh,
        in_specs=placed,
        out_specs=(
            P(("dp", "stream"), None, None),
            P(("dp", "stream"), None, None),
            P(),
            P(),
            P(),
            P(),
            P(),
            P(),
            P(),
            P(),
            P(),
            P(),
            P(),
            P(),
            P(),
            P(),
            P(),
            P(),
            P(),
            P(),
            P(),
            P(),
            P(),
            P(),
            P(),
            P(),
            P(),
            P(),
            P(),
            P(),
            P(),
            P(),
            P(),
            P(),
            P(),
        ),
        check_vma=False,
    )
```

```python
import jax
import jax.numpy as jnp
from jax import lax
from jax.experimental import pallas as pl
from jax.experimental.pallas import tpu as pltpu
from jax.sharding import PartitionSpec as P

HEADS = 8
HEAD = 64
LANES = 128
TILE = 256
EPSILON = 1e-05
AXES = ("dp", "stream")
F32 = jnp.float32
LOW = jnp.bfloat16

(
    GAIN_ONE,
    SHIFT_ONE,
    OFFSET_ONE,
    ATTEND_GAIN,
    ATTEND_SHIFT,
    QUERY_BIAS,
    VALUE_BIAS,
    OUTPUT_BIAS,
    MIXING_GAIN,
    MIXING_SHIFT,
    BATCH_GAIN,
    BATCH_SHIFT,
    SECOND_BIAS,
    GAIN_TWO,
    SHIFT_TWO,
    OFFSET_TWO,
    FINAL_GAIN,
    FINAL_SHIFT,
    FIRST_BIAS,
) = range(19)
TAPS = 20


def nn(a, b):
    return lax.dot_general(a, b, (((1,), (0,)), ((), ())), preferred_element_type=F32)


def nt(a, b):
    return lax.dot_general(a, b, (((1,), (1,)), ((), ())), preferred_element_type=F32)


def tn(a, b):
    return lax.dot_general(a, b, (((0,), (0,)), ((), ())), preferred_element_type=F32)


def column_sum(values):
    return jnp.sum(values, axis=0, keepdims=True)


def sigmoid(values):
    return 0.5 * jnp.tanh(0.5 * values) + 0.5


def normalize(values):
    centred = values - jnp.mean(values, axis=-1, keepdims=True)
    spread = jnp.mean(centred * centred, axis=-1, keepdims=True)
    scale = lax.rsqrt(spread + EPSILON)
    return centred * scale, scale


def norm_backward(grad, gain, unit, scale):
    inner = grad * gain
    middle = jnp.mean(inner, axis=-1, keepdims=True)
    tilt = jnp.mean(inner * unit, axis=-1, keepdims=True)
    return scale * (inner - middle - unit * tilt)


def row_of(table, at, count=1):
    return table[at : at + count, :]


def valid_rows(lengths_ref, step, rows):
    at = lax.broadcasted_iota(jnp.int32, (rows, 1), 0) + step * rows
    return (at < lengths_ref[0]).astype(F32)


def split_three(values):
    high = values.astype(LOW).astype(F32)
    rest = values - high
    middle = rest.astype(LOW).astype(F32)
    return high, middle, rest - middle


def gather_rows(ref, at, rows):
    for offset, row in enumerate(rows):
        ref[at + offset : at + offset + 1, :] += row


def lane_index(rows):
    return lax.broadcasted_iota(jnp.int32, (rows, LANES), 1)


def head_lanes(values, head):
    pair = values[:, (head // 2) * LANES : (head // 2 + 1) * LANES]
    if head % 2 == 1:
        pair = pltpu.roll(pair, HEAD, 1)
    return pair


def join_pair(even, odd):
    lanes = lane_index(even.shape[0])
    return jnp.where(lanes < HEAD, even, pltpu.roll(odd, HEAD, 1))


def front_kernel(
    lengths, x, table, lift, expand, reducer, query, key, value,
    normed_a, acted, slope, x1, normed_b, queries, keys, values, sums,
):
    step = pl.program_id(0)

    @pl.when(step == 0)
    def _():
        sums[...] = jnp.zeros_like(sums)

    rows = x.shape[0]
    valid = valid_rows(lengths, step, rows)
    x0 = x[...].astype(F32)
    unit, scale = normalize(x0)
    low = (unit * row_of(table, GAIN_ONE) + row_of(table, SHIFT_ONE)).astype(LOW)
    normed_a[...] = low
    width = 512
    branch = jnp.zeros((rows, x.shape[1]), F32)
    for part in range(expand.shape[1] // width):
        cut = slice(part * width, (part + 1) * width)
        inner = nn(low, expand[:, cut]) + lift[:, cut]
        gate = sigmoid(inner)
        silu = inner * gate
        active = silu.astype(LOW)
        acted[:, cut] = active
        slope[:, cut] = (gate + silu * (1.0 - gate)).astype(LOW)
        branch = branch + nn(active, reducer[cut, :])
    branch = 0.5 * (branch + row_of(table, OFFSET_ONE))
    after = x0 + branch
    x1[...] = after
    gather_rows(sums, 0, [column_sum(valid * after * after), column_sum(valid * branch * branch)])
    unit, scale = normalize(after)
    low = (unit * row_of(table, ATTEND_GAIN) + row_of(table, ATTEND_SHIFT)).astype(LOW)
    normed_b[...] = low
    lanes = lane_index(rows)
    q_all = (nn(low, query[...]) + row_of(table, QUERY_BIAS)).astype(LOW).astype(F32) * HEAD ** (-0.5)
    k_all = nn(low, key[...])
    v_all = nn(low, value[...]) + row_of(table, VALUE_BIAS)
    ones = jnp.where((lanes >= HEAD) & (lanes < HEAD + 4), 1.0, 0.0)
    first = jnp.where(lanes == HEAD, 1.0, 0.0)
    shade = jnp.where(lanes == HEAD, (valid - 1.0) * 1e30, ones)
    for head in range(HEADS):
        queries[head, :, :] = jnp.where(lanes < HEAD, head_lanes(q_all, head), first).astype(LOW)
        keys[head, :, :] = jnp.where(lanes < HEAD, head_lanes(k_all, head), shade).astype(LOW)
        values[head, :, :] = jnp.where(lanes < HEAD, head_lanes(v_all, head), ones).astype(LOW)


def attend_kernel(
    lengths, queries, keys, values, x1, table, output, point,
    again, mixed_wide, mixed, x2, normed_c, gated, gate_out, convolved, moments, sums,
    padded,
):
    step = pl.program_id(0)
    steps = pl.num_programs(0)
    rows = x1.shape[0]
    width = x1.shape[1]

    @pl.when(step == 0)
    def _():
        sums[...] = jnp.zeros_like(sums)
        padded[0:8, :] = jnp.zeros((8, width), F32)
        padded[padded.shape[0] - 8 :, :] = jnp.zeros((8, width), F32)

    valid = valid_rows(lengths, step, rows)
    lanes = lane_index(rows)
    found = []
    for head in range(HEADS):
        query = queries[head, :, :]
        scores = nt(query, keys[head, :, :])
        top = jnp.max(scores, axis=-1, keepdims=True)
        raised = jnp.exp(scores - top).astype(LOW)
        blend = nn(raised, values[head, :, :])
        total = blend[:, HEAD : HEAD + 1]
        found.append(blend * (1.0 / total))
        high, middle, rest = split_three(-(top + jnp.log(total)))
        marked = jnp.where(lanes == HEAD + 1, high, query.astype(F32))
        marked = jnp.where(lanes == HEAD + 2, middle, marked)
        again[head, :, :] = jnp.where(lanes == HEAD + 3, rest, marked).astype(LOW)
    wide = jnp.concatenate(
        [join_pair(found[2 * pair], found[2 * pair + 1]) for pair in range(HEADS // 2)], axis=1
    )
    mixed_wide[...] = wide
    low = wide.astype(LOW)
    mixed[...] = low
    branch = nn(low, output[...]) + row_of(table, OUTPUT_BIAS)
    after = x1[...] + branch
    x2[...] = after
    gather_rows(sums, 0, [column_sum(valid * after * after), column_sum(valid * branch * branch)])
    unit, scale = normalize(after)
    low = (unit * row_of(table, MIXING_GAIN) + row_of(table, MIXING_SHIFT)).astype(LOW)
    normed_c[...] = low
    doubled = nn(low, point[...])
    gate = sigmoid(doubled[:, width:] + row_of(table, FIRST_BIAS + 1))
    passed = (doubled[:, :width] + row_of(table, FIRST_BIAS)) * gate * valid
    gated[...] = passed
    gate_out[...] = gate
    padded[pl.ds(pl.multiple_of(8 + step * rows, 8), rows), :] = passed

    @pl.when(step == steps - 1)
    def _():
        frames = convolved.shape[0]
        chunk = 128
        count = lengths[0].astype(F32)
        summed = jnp.zeros((1, width), F32)
        for part in range(frames // chunk):
            total = jnp.zeros((chunk, width), F32)
            for tap in range(9):
                start = part * chunk + 4 + tap
                total = total + padded[start : start + chunk, :] * row_of(table, TAPS + tap)
            convolved[part * chunk : (part + 1) * chunk, :] = total
            here = lax.broadcasted_iota(jnp.int32, (chunk, 1), 0) + part * chunk < lengths[0]
            summed = summed + column_sum(jnp.where(here, total, 0.0))
        mean = summed / count
        spread = jnp.zeros((1, width), F32)
        for part in range(frames // chunk):
            here = lax.broadcasted_iota(jnp.int32, (chunk, 1), 0) + part * chunk < lengths[0]
            apart = jnp.where(here, convolved[part * chunk : (part + 1) * chunk, :] - mean, 0.0)
            spread = spread + column_sum(apart * apart)
        moments[...] = jnp.zeros_like(moments)
        moments[0:1, :] = jnp.full((1, width), count, F32)
        moments[1:2, :] = summed
        moments[2:3, :] = spread


def rear_kernel(
    lengths, convolved, x2, cotangent, moments, table, lift, second, expand, reducer,
    block_output, acted_c, low_c, acted, half_low, normed_d, inner_low, stream, direct, sums, wide_sums,
):
    step = pl.program_id(0)

    @pl.when(step == 0)
    def _():
        sums[...] = jnp.zeros_like(sums)
        wide_sums[...] = jnp.zeros_like(wide_sums)

    rows = x2.shape[0]
    valid = valid_rows(lengths, step, rows)
    mean = moments[1:2, :] / moments[0:1, :]
    inverse = lax.rsqrt(moments[2:3, :] / moments[0:1, :] + EPSILON)
    unit_c = (convolved[...] - mean) * inverse
    normal = unit_c * row_of(table, BATCH_GAIN) + row_of(table, BATCH_SHIFT)
    gate = sigmoid(normal)
    silu = normal * gate
    slope_c = gate + silu * (1.0 - gate)
    active_c = silu.astype(LOW)
    acted_c[...] = active_c
    branch = nn(active_c, second[...]) + row_of(table, SECOND_BIAS)
    x3 = x2[...] + branch
    squares = [column_sum(valid * x3 * x3), column_sum(valid * branch * branch)]
    unit_d, scale_d = normalize(x3)
    low_d = (unit_d * row_of(table, GAIN_TWO) + row_of(table, SHIFT_TWO)).astype(LOW)
    normed_d[...] = low_d
    width = 512
    parts = expand.shape[1] // width
    branch = jnp.zeros_like(x3)
    slopes = []
    for part in range(parts):
        cut = slice(part * width, (part + 1) * width)
        inner = nn(low_d, expand[:, cut]) + lift[:, cut]
        gate = sigmoid(inner)
        silu = inner * gate
        active = silu.astype(LOW)
        acted[:, cut] = active
        slopes.append((gate + silu * (1.0 - gate)).astype(LOW))
        branch = branch + nn(active, reducer[cut, :])
    branch = 0.5 * (branch + row_of(table, OFFSET_TWO))
    x4 = x3 + branch
    squares += [column_sum(valid * x4 * x4), column_sum(valid * branch * branch)]
    unit, scale = normalize(x4)
    gain = row_of(table, FINAL_GAIN)
    block_output[...] = (valid * (unit * gain + row_of(table, FINAL_SHIFT))).astype(LOW)
    grad = cotangent[...].astype(F32) * valid
    closing = [column_sum(grad * unit), column_sum(grad)]
    g4 = norm_backward(grad, gain, unit, scale)
    low = (0.5 * g4).astype(LOW)
    half_low[...] = low
    back = jnp.zeros_like(x3)
    for part in range(parts):
        cut = slice(part * width, (part + 1) * width)
        inner = (nt(low, reducer[cut, :]) * slopes[part].astype(F32)).astype(LOW)
        inner_low[:, cut] = inner
        wide_sums[part : part + 1, :] += column_sum(inner.astype(F32))
        back = back + nt(inner, expand[:, cut])
    second_sums = [column_sum(back * unit_d), column_sum(back), column_sum(low.astype(F32))]
    g3 = g4 + norm_backward(back, row_of(table, GAIN_TWO), unit_d, scale_d)
    stream[...] = g3
    low = g3.astype(LOW)
    low_c[...] = low
    grad = nt(low, second[...]) * slope_c
    direct[...] = grad * (row_of(table, BATCH_GAIN) * inverse)
    gather_rows(
        sums,
        0,
        [column_sum(grad), column_sum(grad * unit_c), column_sum(low.astype(F32))]
        + second_sums
        + closing
        + squares,
    )


def weight_kernel(pairs):
    def kernel(*refs):
        for at in range(pairs):
            refs[2 * pairs + at][...] = tn(refs[2 * at][...], refs[2 * at + 1][...])

    return kernel


def mixing_kernel(
    lengths, moments, batch_sums, direct, convolved, gated, gate, x2, stream, mixed_wide, table, point, output,
    doubled_low, stream_out, out_low, grads, sums,
    padded,
):
    step = pl.program_id(0)
    rows = x2.shape[0]
    width = x2.shape[1]
    frames = direct.shape[0]

    @pl.when(step == 0)
    def _():
        sums[...] = jnp.zeros_like(sums)
        count = moments[0:1, :]
        mean = moments[1:2, :] / count
        inverse = lax.rsqrt(moments[2:3, :] / count + EPSILON)
        weight = row_of(table, BATCH_GAIN) * inverse
        mean_grad = -weight * batch_sums[0:1, :] / count
        var_grad = -(inverse * weight) * batch_sums[1:2, :] / count
        padded[0:8, :] = jnp.zeros((8, width), F32)
        padded[padded.shape[0] - 8 :, :] = jnp.zeros((8, width), F32)
        for part in range(frames // rows):
            cut = slice(part * rows, (part + 1) * rows)
            here = lax.broadcasted_iota(jnp.int32, (rows, 1), 0) + part * rows < lengths[0]
            extra = mean_grad + var_grad * (convolved[cut, :] - mean)
            padded[8 + part * rows : 8 + (part + 1) * rows, :] = direct[cut, :] + jnp.where(here, extra, 0.0)

    valid = valid_rows(lengths, step, rows)
    passed = gated[...]
    base = pl.multiple_of(step * rows, 8)
    grad = jnp.zeros((rows, width), F32)
    window = padded[pl.ds(base, rows + 16), :]
    tap_sums = []
    for tap in range(9):
        shifted = window[12 - tap : 12 - tap + rows, :]
        grad = grad + shifted * row_of(table, TAPS + tap)
        tap_sums.append(column_sum(shifted * passed))
    grad = grad * valid
    opened = gate[...]
    left = (grad * opened).astype(LOW)
    right = (grad * passed * (1.0 - opened)).astype(LOW)
    doubled_low[:, :width] = left
    doubled_low[:, width:] = right
    unit, scale = normalize(x2[...])
    back = nt(left, point[:, :width]) + nt(right, point[:, width:])
    g2 = stream[...] + norm_backward(back, row_of(table, MIXING_GAIN), unit, scale)
    stream_out[...] = g2
    low = g2.astype(LOW)
    out_low[...] = low
    gather_rows(
        sums,
        0,
        [
            column_sum(back * unit),
            column_sum(back),
            column_sum(left.astype(F32)),
            column_sum(right.astype(F32)),
        ]
        + tap_sums
        + [column_sum(low.astype(F32))],
    )
    grad_mixed = nt(low, output[...]).astype(LOW).astype(F32)
    product = grad_mixed * mixed_wide[...]
    lanes = lane_index(rows)
    for head in range(HEADS):
        pair = product[:, (head // 2) * LANES : (head // 2 + 1) * LANES]
        mine = (lanes < HEAD) if head % 2 == 0 else (lanes >= HEAD)
        inner = jnp.sum(jnp.where(mine, pair, 0.0), axis=-1, keepdims=True)
        high, middle, rest = split_three(-inner)
        marked = jnp.where(lanes < HEAD, head_lanes(grad_mixed, head), 0.0)
        marked = jnp.where(lanes == HEAD + 1, high, marked)
        marked = jnp.where(lanes == HEAD + 2, middle, marked)
        grads[head, :, :] = jnp.where(lanes == HEAD + 3, rest, marked).astype(LOW)


def attend_back_kernel(queries, keys, values, grads, query_grad, key_grad, value_grad):
    frames = queries.shape[1]
    chunk = 256
    turned = []
    for side in range(2):
        query = queries[side, :, :]
        grad = grads[side, :, :]
        total = jnp.zeros((LANES, frames), F32)
        key_parts = []
        value_parts = []
        for part in range(frames // chunk):
            cut = slice(part * chunk, (part + 1) * chunk)
            key = keys[side, cut, :]
            softened = jnp.exp(nt(key, query))
            value_parts.append(nn(softened.astype(LOW), grad))
            low = (softened * nt(values[side, cut, :], grad)).astype(LOW)
            key_parts.append(nn(low, query))
            total = total + tn(key, low)
        turned.append((total[0:HEAD, :], key_parts, value_parts))
    both = jnp.concatenate([turned[0][0], turned[1][0]], axis=0) * HEAD ** (-0.5)
    query_grad[...] = both.T.astype(LOW)
    for part in range(frames // chunk):
        cut = slice(part * chunk, (part + 1) * chunk)
        key_grad[cut, :] = join_pair(turned[0][1][part], turned[1][1][part]).astype(LOW)
        value_grad[cut, :] = join_pair(turned[0][2][part], turned[1][2][part]).astype(LOW)


def first_back_kernel(
    query_grad, key_grad, value_grad, x1, stream, slope, table, query, key, value, reducer,
    stream_out, half_low, inner_low, sums, wide_sums,
):
    step = pl.program_id(0)

    @pl.when(step == 0)
    def _():
        sums[...] = jnp.zeros_like(sums)
        wide_sums[...] = jnp.zeros_like(wide_sums)

    unit, scale = normalize(x1[...])
    back = nt(query_grad[...], query[...]) + nt(key_grad[...], key[...]) + nt(value_grad[...], value[...])
    g1 = stream[...] + norm_backward(back, row_of(table, ATTEND_GAIN), unit, scale)
    stream_out[...] = g1
    low = (0.5 * g1).astype(LOW)
    half_low[...] = low
    gather_rows(
        sums,
        0,
        [
            column_sum(back * unit),
            column_sum(back),
            column_sum(query_grad[...].astype(F32)),
            column_sum(value_grad[...].astype(F32)),
            column_sum(low.astype(F32)),
        ],
    )
    width = 512
    for part in range(slope.shape[1] // width):
        cut = slice(part * width, (part + 1) * width)
        inner = (nt(low, reducer[cut, :]) * slope[:, cut].astype(F32)).astype(LOW)
        inner_low[:, cut] = inner
        wide_sums[part : part + 1, :] += column_sum(inner.astype(F32))


def input_kernel(inner_low, x, stream, table, expand, input_gradient, sums):
    step = pl.program_id(0)

    @pl.when(step == 0)
    def _():
        sums[...] = jnp.zeros_like(sums)

    unit, scale = normalize(x[...].astype(F32))
    back = nt(inner_low[...], expand[...])
    gather_rows(sums, 0, [column_sum(back * unit), column_sum(back)])
    g0 = stream[...] + norm_backward(back, row_of(table, GAIN_ONE), unit, scale)
    input_gradient[...] = g0.astype(LOW)


def whole(array):
    return pl.BlockSpec(array.shape, lambda step: (0,) * len(array.shape))


def tiled(array):
    if len(array.shape) == 3:
        return pl.BlockSpec((array.shape[0], TILE, array.shape[2]), lambda step: (0, step, 0))
    return pl.BlockSpec((TILE, array.shape[1]), lambda step: (step, 0))


SCALAR = pl.BlockSpec(memory_space=pltpu.SMEM)


def shaped(dims, dtype):
    return jax.ShapeDtypeStruct(dims, dtype)


def call(kernel, steps, operands, results, scratch=(), flops=0, limit=56):
    arrays = [array for array, spec in operands]
    moved = sum(array.size * array.dtype.itemsize for array in arrays)
    moved += sum(array.size * array.dtype.itemsize for array, spec in results)
    return pl.pallas_call(
        kernel,
        grid=(steps,),
        in_specs=[spec if isinstance(spec, pl.BlockSpec) else spec(array) for array, spec in operands],
        out_specs=[spec if isinstance(spec, pl.BlockSpec) else spec(array) for array, spec in results],
        out_shape=[array for array, spec in results],
        scratch_shapes=list(scratch),
        compiler_params=pltpu.CompilerParams(vmem_limit_bytes=limit << 20),
        cost_estimate=pl.CostEstimate(flops=flops, bytes_accessed=moved, transcendentals=0),
    )(*arrays)


def weight_grads(pairs, steps=4):
    operands = []
    results = []
    flops = 0
    for left, right in pairs:
        rows = left.shape[1] // steps
        operands.append((left, pl.BlockSpec((left.shape[0], rows), lambda step: (0, step))))
        operands.append((right, whole))
        results.append(
            (
                shaped((left.shape[1], right.shape[1]), F32),
                pl.BlockSpec((rows, right.shape[1]), lambda step: (step, 0)),
            )
        )
        flops += 2 * left.shape[0] * left.shape[1] * right.shape[1]
    return call(weight_kernel(len(pairs)), steps, operands, results, flops=flops)


def bits_of(axis):
    return lax.axis_size(axis).bit_length() - 1


def exchange(values, axis, bit):
    count = lax.axis_size(axis)
    return lax.ppermute(values, axis, [(at, at ^ (1 << bit)) for at in range(count)])


def own_bit(axis, bit):
    return (lax.axis_index(axis) >> bit) & 1


def every_bit():
    return [(axis, bit) for axis in AXES for bit in range(bits_of(axis))]


def halve(values, axis, bit):
    half = values.shape[0] // 2
    mine = own_bit(axis, bit)
    arrived = exchange(lax.dynamic_slice_in_dim(values, (1 - mine) * half, half), axis, bit)
    return lax.dynamic_slice_in_dim(values, mine * half, half) + arrived


def double(values, axis, bit):
    arrived = exchange(values, axis, bit)
    upper = own_bit(axis, bit) == 1
    return jnp.concatenate([jnp.where(upper, arrived, values), jnp.where(upper, values, arrived)])


def part_orders():
    pair = every_bit()[0]
    rest_dp = [step for step in every_bit()[1:] if step[0] == "dp"]
    rest_stream = [step for step in every_bit() if step[0] == "stream"]
    return [
        [pair] + rest_dp + rest_stream,
        [pair] + rest_dp[::-1] + rest_stream,
        [pair] + rest_stream + rest_dp,
    ]


def sum_parts(parts):
    orders = part_orders()
    steps = len(orders[0])
    for at in range(steps):
        parts = [halve(part, *orders[which % 3][at]) for which, part in enumerate(parts)]
    for at in reversed(range(steps)):
        parts = [double(part, *orders[which % 3][at]) for which, part in enumerate(parts)]
    return parts


def sum_small(values):
    for axis, bit in every_bit():
        values = values + exchange(values, axis, bit)
    return values


def join_moments(packed):
    for axis, bit in every_bit():
        other = exchange(packed, axis, bit)
        both = packed + other
        gap = packed[1] / packed[0] - other[1] / other[0]
        extra = gap * gap * (packed[0] * other[0] / both[0])
        packed = jnp.concatenate([both[0:2], both[2:3] + extra[None], both[3:]])
    return packed


def body(
    inputs, lengths, cotangent,
    gain_one, shift_one, expand_one, lift_one, reduce_one, offset_one,
    attend_gain, attend_shift, query_proj, query_bias, key_proj, value_proj, value_bias, output_proj, output_bias,
    mixing_gain, mixing_shift, point_first, first_bias, depth_kernel, batch_gain, batch_shift, point_second, second_bias,
    gain_two, shift_two, expand_two, lift_two, reduce_two, offset_two, final_gain, final_shift,
):
    utterances, frames, width = inputs.shape
    hidden = expand_one.shape[1]
    steps = frames // TILE
    x = inputs.reshape(frames, width)
    cotangent_rows = cotangent.reshape(frames, width)
    table = jnp.concatenate(
        [
            vector.reshape(-1, width)
            for vector in (
                gain_one, shift_one, offset_one, attend_gain, attend_shift, query_bias, value_bias, output_bias,
                mixing_gain, mixing_shift, batch_gain, batch_shift, second_bias, gain_two, shift_two, offset_two,
                final_gain, final_shift, first_bias, depth_kernel,
            )
        ]
    ).astype(F32)
    table = jnp.pad(table, ((0, 32 - table.shape[0]), (0, 0)))
    lift_first = lift_one.astype(F32).reshape(1, hidden)
    lift_second = lift_two.astype(F32).reshape(1, hidden)
    rows_low = shaped((frames, width), LOW)
    rows_full = shaped((frames, width), F32)
    hidden_low = shaped((frames, hidden), LOW)
    heads_low = shaped((HEADS, frames, LANES), LOW)

    def small(rows):
        return (shaped((rows, width), F32), whole)

    normed_a, acted_a, slope_a, x1, normed_b, queries, keys, values, sums_a = call(
        front_kernel,
        steps,
        [
            (lengths, SCALAR), (x, tiled), (table, whole), (lift_first, whole), (expand_one, whole),
            (reduce_one, whole), (query_proj, whole), (key_proj, whole), (value_proj, whole),
        ],
        [
            (rows_low, tiled), (hidden_low, tiled), (hidden_low, tiled), (rows_full, tiled), (rows_low, tiled),
            (heads_low, tiled), (heads_low, tiled), (heads_low, tiled), small(8),
        ],
        flops=2 * frames * width * (2 * hidden + 3 * width),
    )
    again, mixed_wide, mixed, x2, normed_c, gated, gate_c, convolved, moments, sums_b = call(
        attend_kernel,
        steps,
        [
            (lengths, SCALAR), (queries, tiled), (keys, whole), (values, whole), (x1, tiled), (table, whole),
            (output_proj, whole), (point_first, whole),
        ],
        [
            (heads_low, tiled), (rows_full, tiled), (rows_low, tiled), (rows_full, tiled), (rows_low, tiled),
            (rows_full, tiled), (rows_full, tiled), (rows_full, whole), small(8), small(8),
        ],
        scratch=[pltpu.VMEM((frames + 16, width), F32)],
        flops=8 * frames * frames * width,
    )
    moments = join_moments(moments)
    (
        block_output, acted_c, low_c, acted_d, half_d, normed_d, inner_d, g3, direct, sums_c, lift_two_sums,
    ) = call(
        rear_kernel,
        steps,
        [
            (lengths, SCALAR), (convolved, tiled), (x2, tiled), (cotangent_rows, tiled), (moments, whole),
            (table, whole), (lift_second, whole), (point_second, whole), (expand_two, whole), (reduce_two, whole),
        ],
        [
            (rows_low, tiled), (rows_low, tiled), (rows_low, tiled), (hidden_low, tiled), (rows_low, tiled),
            (rows_low, tiled), (hidden_low, tiled), (rows_full, tiled), (rows_full, tiled), small(16), small(8),
        ],
        flops=2 * frames * width * (4 * hidden + 2 * width),
    )
    batch_sums = sum_small(sums_c[0:8])
    grad_reduce_two, grad_expand_two, grad_second = weight_grads(
        [(acted_d, half_d), (normed_d, inner_d), (acted_c, low_c)]
    )
    second_large = lax.psum((grad_expand_two, grad_reduce_two), AXES)
    doubled_low, g2, out_low, mixed_grads, sums_d = call(
        mixing_kernel,
        steps,
        [
            (lengths, SCALAR), (moments, whole), (batch_sums, whole), (direct, whole), (convolved, whole),
            (gated, tiled), (gate_c, tiled), (x2, tiled), (g3, tiled), (mixed_wide, tiled), (table, whole),
            (point_first, whole), (output_proj, whole),
        ],
        [
            (shaped((frames, 2 * width), LOW), tiled), (rows_full, tiled), (rows_low, tiled), (heads_low, tiled),
            small(16),
        ],
        scratch=[pltpu.VMEM((frames + 16, width), F32)],
        flops=2 * frames * width * 3 * width,
    )
    grad_point_first, grad_output = weight_grads([(normed_c, doubled_low), (mixed, out_low)])
    pair_block = pl.BlockSpec((2, frames, LANES), lambda step: (step, 0, 0))
    lane_block = pl.BlockSpec((frames, LANES), lambda step: (0, step))
    query_grad, key_grad, value_grad = call(
        attend_back_kernel,
        HEADS // 2,
        [(again, pair_block), (keys, pair_block), (values, pair_block), (mixed_grads, pair_block)],
        [(rows_low, lane_block), (rows_low, lane_block), (rows_low, lane_block)],
        flops=20 * frames * frames * width,
    )
    g1, half_a, inner_a, sums_e, lift_one_sums = call(
        first_back_kernel,
        steps,
        [
            (query_grad, tiled), (key_grad, tiled), (value_grad, tiled), (x1, tiled), (g2, tiled), (slope_a, tiled),
            (table, whole), (query_proj, whole), (key_proj, whole), (value_proj, whole), (reduce_one, whole),
        ],
        [(rows_full, tiled), (rows_low, tiled), (hidden_low, tiled), small(8), small(8)],
        flops=2 * frames * width * (hidden + 3 * width),
    )
    grad_query, grad_key, grad_value = weight_grads(
        [(normed_b, query_grad), (normed_b, key_grad), (normed_b, value_grad)]
    )
    grad_reduce_one, grad_expand_one = weight_grads([(acted_a, half_a), (normed_a, inner_a)])
    input_gradient, sums_f = call(
        input_kernel,
        steps,
        [(inner_a, tiled), (x, tiled), (g1, tiled), (table, whole), (expand_one, whole)],
        [(rows_low, tiled), small(8)],
        flops=2 * frames * width * hidden,
    )
    large = jnp.concatenate(
        [
            grad_point_first[:, :width], grad_point_first[:, width:], grad_second, grad_query, grad_key, grad_value,
            grad_output, sums_a, sums_b, sums_c, lift_two_sums, sums_d, jnp.zeros((72, width), F32),
        ]
    )
    cut = 1408
    middle = jnp.concatenate(sum_parts([large[:cut], large[cut : 2 * cut], large[2 * cut :]]))
    first_reduce, first_expand = sum_parts([grad_reduce_one, grad_expand_one])
    late = sum_small(jnp.concatenate([sums_e, lift_one_sums, sums_f]))
    tail = middle[7 * width :]
    total_a, total_b, total_c, total_lift, total_d = (
        tail[0:8], tail[8:16], tail[16:32], tail[32:40], tail[40:56],
    )
    total_e, total_lift_one, total_f = late[0:8], late[8:16], late[16:24]
    squares = jnp.sum(
        jnp.stack(
            [
                total_a[0], total_b[0], total_c[8], total_c[10], total_a[1], total_b[1], total_c[9], total_c[11],
            ]
        ),
        axis=1,
    )
    rms_stats = jnp.sqrt(squares / (moments[0, 0] * width))

    def block(at):
        return middle[at * width : (at + 1) * width]

    return (
        block_output.reshape(inputs.shape),
        input_gradient.reshape(inputs.shape),
        total_f[0],
        total_f[1],
        first_expand,
        total_lift_one[0 : hidden // width].reshape(-1),
        first_reduce,
        total_e[4],
        total_e[0],
        total_e[1],
        block(3),
        total_e[2],
        block(4),
        block(5),
        total_e[3],
        block(6),
        total_d[13],
        total_d[0],
        total_d[1],
        jnp.concatenate([block(0), block(1)], axis=1),
        total_d[2:4].reshape(-1),
        total_d[4:13],
        batch_sums[1],
        batch_sums[0],
        block(2),
        total_c[2],
        total_c[3],
        total_c[4],
        second_large[0],
        total_lift[0 : hidden // width].reshape(-1),
        second_large[1],
        total_c[5],
        total_c[6],
        total_c[7],
        rms_stats,
    )


def solution(mesh):
    rows = P(AXES, None, None)
    return jax.shard_map(
        body,
        mesh=mesh,
        in_specs=(rows, P(AXES), rows) + (P(),) * 32,
        out_specs=(rows, rows) + (P(),) * 33,
        check_vma=False,
    )
```

```python
import jax
import jax.numpy as jnp
from jax import lax
from jax.experimental import pallas as pl
from jax.experimental.pallas import tpu as pltpu
from jax.sharding import PartitionSpec as P

HEADS = 8
HEAD = 64
LANES = 128
TILE = 512
EPSILON = 1e-05
AXES = ("dp", "stream")
STAGE_FLOPS = 100_000_000_000
STAGE_LIMIT = 24
F32 = jnp.float32
LOW = jnp.bfloat16

(
    GAIN_ONE,
    SHIFT_ONE,
    OFFSET_ONE,
    ATTEND_GAIN,
    ATTEND_SHIFT,
    QUERY_BIAS,
    VALUE_BIAS,
    OUTPUT_BIAS,
    MIXING_GAIN,
    MIXING_SHIFT,
    BATCH_GAIN,
    BATCH_SHIFT,
    SECOND_BIAS,
    GAIN_TWO,
    SHIFT_TWO,
    OFFSET_TWO,
    FINAL_GAIN,
    FINAL_SHIFT,
    FIRST_BIAS,
) = range(19)
TAPS = 20


def nn(a, b):
    return lax.dot_general(a, b, (((1,), (0,)), ((), ())), preferred_element_type=F32)


def nt(a, b):
    return lax.dot_general(a, b, (((1,), (1,)), ((), ())), preferred_element_type=F32)


def tn(a, b):
    return lax.dot_general(a, b, (((0,), (0,)), ((), ())), preferred_element_type=F32)


def column_sum(values):
    return jnp.sum(values, axis=0, keepdims=True)


def sigmoid(values):
    return 0.5 * jnp.tanh(0.5 * values) + 0.5


def normalize(values):
    centred = values - jnp.mean(values, axis=-1, keepdims=True)
    spread = jnp.mean(centred * centred, axis=-1, keepdims=True)
    scale = lax.rsqrt(spread + EPSILON)
    return centred * scale, scale


def norm_backward(grad, gain, unit, scale):
    inner = grad * gain
    middle = jnp.mean(inner, axis=-1, keepdims=True)
    tilt = jnp.mean(inner * unit, axis=-1, keepdims=True)
    return scale * (inner - middle - unit * tilt)


def row_of(table, at, count=1):
    return table[at : at + count, :]


def valid_rows(lengths_ref, step, rows):
    at = lax.broadcasted_iota(jnp.int32, (rows, 1), 0) + step * rows
    return (at < lengths_ref[0]).astype(F32)


def split_three(values):
    high = values.astype(LOW).astype(F32)
    rest = values - high
    middle = rest.astype(LOW).astype(F32)
    return high, middle, rest - middle


def gather_rows(ref, at, rows):
    for offset, row in enumerate(rows):
        ref[at + offset : at + offset + 1, :] += row


def lane_index(rows):
    return lax.broadcasted_iota(jnp.int32, (rows, LANES), 1)


def head_lanes(values, head):
    pair = values[:, (head // 2) * LANES : (head // 2 + 1) * LANES]
    if head % 2 == 1:
        pair = pltpu.roll(pair, HEAD, 1)
    return pair


def join_pair(even, odd):
    lanes = lane_index(even.shape[0])
    return jnp.where(lanes < HEAD, even, pltpu.roll(odd, HEAD, 1))


def table_kernel(*refs):
    table, lift_first, lift_second = refs[-3:]
    width = table.shape[1]
    for at in range(FIRST_BIAS):
        table[at : at + 1, :] = refs[at][...].astype(F32).reshape(1, width)
    table[FIRST_BIAS : FIRST_BIAS + 2, :] = refs[FIRST_BIAS][...].astype(F32).reshape(2, width)
    table[TAPS : TAPS + 9, :] = refs[FIRST_BIAS + 1][...].astype(F32)
    table[TAPS + 9 :, :] = jnp.zeros((table.shape[0] - TAPS - 9, width), F32)
    lift_first[...] = refs[FIRST_BIAS + 2][...].astype(F32).reshape(lift_first.shape)
    lift_second[...] = refs[FIRST_BIAS + 3][...].astype(F32).reshape(lift_second.shape)


def forward_kernel(
    lengths, x, table, lift, expand, reducer, query, key, value, output, point,
    normed_a, acted, slope, x1, normed_b, keys, values,
    again, mixed_wide, mixed, x2, normed_c, gated, gate_out, convolved, moments, sums,
    all_queries, all_keys, all_values, stream, padded,
):
    step = pl.program_id(0)
    rows = x.shape[0]
    width = x.shape[1]
    tiles = stream.shape[0] // rows

    @pl.when(step == 0)
    def _():
        sums[...] = jnp.zeros_like(sums)
        padded[0:8, :] = jnp.zeros((8, width), F32)
        padded[padded.shape[0] - 8 :, :] = jnp.zeros((8, width), F32)

    lanes = lane_index(rows)

    @pl.when(step < tiles)
    def _():
        valid = valid_rows(lengths, step, rows)
        here = pl.ds(pl.multiple_of(step * rows, rows), rows)
        x0 = x[...].astype(F32)
        unit, scale = normalize(x0)
        low = (unit * row_of(table, GAIN_ONE) + row_of(table, SHIFT_ONE)).astype(LOW)
        normed_a[...] = low
        part_width = 512
        branch = jnp.zeros((rows, width), F32)
        for part in range(expand.shape[1] // part_width):
            cut = slice(part * part_width, (part + 1) * part_width)
            inner = nn(low, expand[:, cut]) + lift[:, cut]
            gate = sigmoid(inner)
            silu = inner * gate
            active = silu.astype(LOW)
            acted[:, cut] = active
            slope[:, cut] = (gate + silu * (1.0 - gate)).astype(LOW)
            branch = branch + nn(active, reducer[cut, :])
        branch = 0.5 * (branch + row_of(table, OFFSET_ONE))
        after = x0 + branch
        x1[...] = after
        stream[here, :] = after
        gather_rows(sums, 0, [column_sum(valid * after * after), column_sum(valid * branch * branch)])
        unit, scale = normalize(after)
        low = (unit * row_of(table, ATTEND_GAIN) + row_of(table, ATTEND_SHIFT)).astype(LOW)
        normed_b[...] = low
        q_all = (nn(low, query[...]) + row_of(table, QUERY_BIAS)).astype(LOW).astype(F32) * HEAD ** (-0.5)
        k_all = nn(low, key[...])
        v_all = nn(low, value[...]) + row_of(table, VALUE_BIAS)
        ones = jnp.where((lanes >= HEAD) & (lanes < HEAD + 4), 1.0, 0.0)
        first = jnp.where(lanes == HEAD, 1.0, 0.0)
        shade = jnp.where(lanes == HEAD, (valid - 1.0) * 1e30, ones)
        for head in range(HEADS):
            all_queries[head, here, :] = jnp.where(lanes < HEAD, head_lanes(q_all, head), first).astype(LOW)
            marked = jnp.where(lanes < HEAD, head_lanes(k_all, head), shade).astype(LOW)
            keys[head, :, :] = marked
            all_keys[head, here, :] = marked
            marked = jnp.where(lanes < HEAD, head_lanes(v_all, head), ones).astype(LOW)
            values[head, :, :] = marked
            all_values[head, here, :] = marked

    @pl.when(step >= tiles)
    def _():
        tile = step - tiles
        valid = valid_rows(lengths, tile, rows)
        here = pl.ds(pl.multiple_of(tile * rows, rows), rows)
        found = []
        for head in range(HEADS):
            query = all_queries[head, here, :]
            scores = nt(query, all_keys[head, :, :])
            top = jnp.max(scores, axis=-1, keepdims=True)
            raised = jnp.exp(scores - top).astype(LOW)
            blend = nn(raised, all_values[head, :, :])
            total = blend[:, HEAD : HEAD + 1]
            found.append(blend * (1.0 / total))
            high, middle, rest = split_three(-(top + jnp.log(total)))
            marked = jnp.where(lanes == HEAD + 1, high, query.astype(F32))
            marked = jnp.where(lanes == HEAD + 2, middle, marked)
            again[head, :, :] = jnp.where(lanes == HEAD + 3, rest, marked).astype(LOW)
        wide = jnp.concatenate(
            [join_pair(found[2 * pair], found[2 * pair + 1]) for pair in range(HEADS // 2)], axis=1
        )
        mixed_wide[...] = wide
        low = wide.astype(LOW)
        mixed[...] = low
        branch = nn(low, output[...]) + row_of(table, OUTPUT_BIAS)
        after = stream[here, :] + branch
        x2[...] = after
        gather_rows(sums, 2, [column_sum(valid * after * after), column_sum(valid * branch * branch)])
        unit, scale = normalize(after)
        low = (unit * row_of(table, MIXING_GAIN) + row_of(table, MIXING_SHIFT)).astype(LOW)
        normed_c[...] = low
        doubled = nn(low, point[...])
        gate = sigmoid(doubled[:, width:] + row_of(table, FIRST_BIAS + 1))
        passed = (doubled[:, :width] + row_of(table, FIRST_BIAS)) * gate * valid
        gated[...] = passed
        gate_out[...] = gate
        padded[pl.ds(pl.multiple_of(8 + tile * rows, 8), rows), :] = passed

    @pl.when(step == pl.num_programs(0) - 1)
    def _():
        frames = convolved.shape[0]
        chunk = 128
        count = lengths[0].astype(F32)
        summed = jnp.zeros((1, width), F32)
        for part in range(frames // chunk):
            total = jnp.zeros((chunk, width), F32)
            for tap in range(9):
                start = part * chunk + 4 + tap
                total = total + padded[start : start + chunk, :] * row_of(table, TAPS + tap)
            convolved[part * chunk : (part + 1) * chunk, :] = total
            here = lax.broadcasted_iota(jnp.int32, (chunk, 1), 0) + part * chunk < lengths[0]
            summed = summed + column_sum(jnp.where(here, total, 0.0))
        mean = summed / count
        spread = jnp.zeros((1, width), F32)
        for part in range(frames // chunk):
            here = lax.broadcasted_iota(jnp.int32, (chunk, 1), 0) + part * chunk < lengths[0]
            apart = jnp.where(here, convolved[part * chunk : (part + 1) * chunk, :] - mean, 0.0)
            spread = spread + column_sum(apart * apart)
        moments[...] = jnp.zeros_like(moments)
        moments[0:1, :] = jnp.full((1, width), count, F32)
        moments[1:2, :] = summed
        moments[2:3, :] = spread


def rear_kernel(
    lengths, convolved, x2, cotangent, moments, table, lift, second, expand, reducer,
    block_output, stream, direct, grad_reduce, grad_expand, grad_second, sums, wide_sums,
    all_acted_c, all_low_c, all_acted, all_half, all_normed, all_inner,
):
    step = pl.program_id(0)

    @pl.when(step == 0)
    def _():
        sums[...] = jnp.zeros_like(sums)
        wide_sums[...] = jnp.zeros_like(wide_sums)

    rows = x2.shape[0]
    tiles = all_acted.shape[0] // rows

    @pl.when(step < tiles)
    def _():
        here = pl.ds(pl.multiple_of(step * rows, rows), rows)
        valid = valid_rows(lengths, step, rows)
        mean = moments[1:2, :] / moments[0:1, :]
        inverse = lax.rsqrt(moments[2:3, :] / moments[0:1, :] + EPSILON)
        unit_c = (convolved[...] - mean) * inverse
        normal = unit_c * row_of(table, BATCH_GAIN) + row_of(table, BATCH_SHIFT)
        gate = sigmoid(normal)
        silu = normal * gate
        slope_c = gate + silu * (1.0 - gate)
        active_c = silu.astype(LOW)
        all_acted_c[here, :] = active_c
        branch = nn(active_c, second[...]) + row_of(table, SECOND_BIAS)
        x3 = x2[...] + branch
        squares = [column_sum(valid * x3 * x3), column_sum(valid * branch * branch)]
        unit_d, scale_d = normalize(x3)
        low_d = (unit_d * row_of(table, GAIN_TWO) + row_of(table, SHIFT_TWO)).astype(LOW)
        all_normed[here, :] = low_d
        width = 512
        parts = expand.shape[1] // width
        branch = jnp.zeros_like(x3)
        slopes = []
        for part in range(parts):
            cut = slice(part * width, (part + 1) * width)
            inner = nn(low_d, expand[:, cut]) + lift[:, cut]
            gate = sigmoid(inner)
            silu = inner * gate
            active = silu.astype(LOW)
            all_acted[here, cut] = active
            slopes.append((gate + silu * (1.0 - gate)).astype(LOW))
            branch = branch + nn(active, reducer[cut, :])
        branch = 0.5 * (branch + row_of(table, OFFSET_TWO))
        x4 = x3 + branch
        squares += [column_sum(valid * x4 * x4), column_sum(valid * branch * branch)]
        unit, scale = normalize(x4)
        gain = row_of(table, FINAL_GAIN)
        block_output[...] = (valid * (unit * gain + row_of(table, FINAL_SHIFT))).astype(LOW)
        grad = cotangent[...].astype(F32) * valid
        closing = [column_sum(grad * unit), column_sum(grad)]
        g4 = norm_backward(grad, gain, unit, scale)
        low = (0.5 * g4).astype(LOW)
        all_half[here, :] = low
        back = jnp.zeros_like(x3)
        for part in range(parts):
            cut = slice(part * width, (part + 1) * width)
            inner = (nt(low, reducer[cut, :]) * slopes[part].astype(F32)).astype(LOW)
            all_inner[here, cut] = inner
            wide_sums[part : part + 1, :] += column_sum(inner.astype(F32))
            back = back + nt(inner, expand[:, cut])
        second_sums = [column_sum(back * unit_d), column_sum(back), column_sum(low.astype(F32))]
        g3 = g4 + norm_backward(back, row_of(table, GAIN_TWO), unit_d, scale_d)
        stream[...] = g3
        low = g3.astype(LOW)
        all_low_c[here, :] = low
        grad = nt(low, second[...]) * slope_c
        direct[...] = grad * (row_of(table, BATCH_GAIN) * inverse)
        gather_rows(
            sums,
            0,
            [column_sum(grad), column_sum(grad * unit_c), column_sum(low.astype(F32))]
            + second_sums
            + closing
            + squares,
        )

    @pl.when(step >= tiles)
    def _():
        part = step - tiles

        def columns(array, count):
            return array[:, pl.ds(pl.multiple_of(part * count, count), count)]

        grad_reduce[...] = tn(columns(all_acted, grad_reduce.shape[0]), all_half[...])
        grad_expand[...] = tn(columns(all_normed, grad_expand.shape[0]), all_inner[...])
        grad_second[...] = tn(columns(all_acted_c, grad_second.shape[0]), all_low_c[...])


def mixing_kernel(
    lengths, moments, batch_sums, direct, convolved, gated, gate, x2, stream, mixed_wide, table, point, output, normed, mixed,
    stream_out, grads, grad_point, grad_output, sums,
    padded, all_doubled, all_out,
):
    step = pl.program_id(0)
    rows = x2.shape[0]
    width = x2.shape[1]
    frames = direct.shape[0]

    @pl.when(step == 0)
    def _():
        sums[...] = jnp.zeros_like(sums)
        count = moments[0:1, :]
        mean = moments[1:2, :] / count
        inverse = lax.rsqrt(moments[2:3, :] / count + EPSILON)
        weight = row_of(table, BATCH_GAIN) * inverse
        mean_grad = -weight * batch_sums[0:1, :] / count
        var_grad = -(inverse * weight) * batch_sums[1:2, :] / count
        padded[0:8, :] = jnp.zeros((8, width), F32)
        padded[padded.shape[0] - 8 :, :] = jnp.zeros((8, width), F32)
        for part in range(frames // rows):
            cut = slice(part * rows, (part + 1) * rows)
            here = lax.broadcasted_iota(jnp.int32, (rows, 1), 0) + part * rows < lengths[0]
            extra = mean_grad + var_grad * (convolved[cut, :] - mean)
            padded[8 + part * rows : 8 + (part + 1) * rows, :] = direct[cut, :] + jnp.where(here, extra, 0.0)

    tiles = frames // rows

    @pl.when(step < tiles)
    def _():
        here = pl.ds(pl.multiple_of(step * rows, rows), rows)
        valid = valid_rows(lengths, step, rows)
        passed = gated[...]
        base = pl.multiple_of(step * rows, 8)
        grad = jnp.zeros((rows, width), F32)
        window = padded[pl.ds(base, rows + 16), :]
        tap_sums = []
        for tap in range(9):
            shifted = window[12 - tap : 12 - tap + rows, :]
            grad = grad + shifted * row_of(table, TAPS + tap)
            tap_sums.append(column_sum(shifted * passed))
        grad = grad * valid
        opened = gate[...]
        left = (grad * opened).astype(LOW)
        right = (grad * passed * (1.0 - opened)).astype(LOW)
        all_doubled[here, :width] = left
        all_doubled[here, width:] = right
        unit, scale = normalize(x2[...])
        back = nt(left, point[:, :width]) + nt(right, point[:, width:])
        g2 = stream[...] + norm_backward(back, row_of(table, MIXING_GAIN), unit, scale)
        stream_out[...] = g2
        low = g2.astype(LOW)
        all_out[here, :] = low
        gather_rows(
            sums,
            0,
            [
                column_sum(back * unit),
                column_sum(back),
                column_sum(left.astype(F32)),
                column_sum(right.astype(F32)),
            ]
            + tap_sums
            + [column_sum(low.astype(F32))],
        )
        grad_mixed = nt(low, output[...]).astype(LOW).astype(F32)
        product = grad_mixed * mixed_wide[...]
        lanes = lane_index(rows)
        for head in range(HEADS):
            pair = product[:, (head // 2) * LANES : (head // 2 + 1) * LANES]
            mine = (lanes < HEAD) if head % 2 == 0 else (lanes >= HEAD)
            inner = jnp.sum(jnp.where(mine, pair, 0.0), axis=-1, keepdims=True)
            high, middle, rest = split_three(-inner)
            marked = jnp.where(lanes < HEAD, head_lanes(grad_mixed, head), 0.0)
            marked = jnp.where(lanes == HEAD + 1, high, marked)
            marked = jnp.where(lanes == HEAD + 2, middle, marked)
            grads[head, :, :] = jnp.where(lanes == HEAD + 3, rest, marked).astype(LOW)

    @pl.when(step >= tiles)
    def _():
        grad_point[...] = tn(normed[...], all_doubled[...])
        grad_output[...] = tn(mixed[...], all_out[...])


def attend_back_kernel(queries, keys, values, grads, query_grad, key_grad, value_grad):
    frames = queries.shape[1]
    chunk = 256
    turned = []
    for side in range(2):
        query = queries[side, :, :]
        grad = grads[side, :, :]
        total = jnp.zeros((LANES, frames), F32)
        key_parts = []
        value_parts = []
        for part in range(frames // chunk):
            cut = slice(part * chunk, (part + 1) * chunk)
            key = keys[side, cut, :]
            softened = jnp.exp(nt(key, query))
            value_parts.append(nn(softened.astype(LOW), grad))
            low = (softened * nt(values[side, cut, :], grad)).astype(LOW)
            key_parts.append(nn(low, query))
            total = total + tn(key, low)
        turned.append((total[0:HEAD, :], key_parts, value_parts))
    both = jnp.concatenate([turned[0][0], turned[1][0]], axis=0) * HEAD ** (-0.5)
    query_grad[...] = both.T.astype(LOW)
    for part in range(frames // chunk):
        cut = slice(part * chunk, (part + 1) * chunk)
        key_grad[cut, :] = join_pair(turned[0][1][part], turned[1][1][part]).astype(LOW)
        value_grad[cut, :] = join_pair(turned[0][2][part], turned[1][2][part]).astype(LOW)


def first_back_kernel(
    query_grad, key_grad, value_grad, x1, stream, slope, table, query, key, value, reducer, acted, normed, normed_b, x, expand,
    input_gradient, grad_reduce, grad_expand, grad_query, grad_key, grad_value, sums, wide_sums,
    all_half, all_inner,
):
    step = pl.program_id(0)

    @pl.when(step == 0)
    def _():
        sums[...] = jnp.zeros_like(sums)
        wide_sums[...] = jnp.zeros_like(wide_sums)

    rows = x1.shape[0]
    tiles = all_half.shape[0] // rows

    @pl.when(step < tiles)
    def _():
        here = pl.ds(pl.multiple_of(step * rows, rows), rows)
        unit, scale = normalize(x1[...])
        back = nt(query_grad[here, :], query[...]) + nt(key_grad[here, :], key[...]) + nt(value_grad[here, :], value[...])
        g1 = stream[...] + norm_backward(back, row_of(table, ATTEND_GAIN), unit, scale)
        low = (0.5 * g1).astype(LOW)
        all_half[here, :] = low
        gather_rows(
            sums,
            0,
            [
                column_sum(back * unit),
                column_sum(back),
                column_sum(query_grad[here, :].astype(F32)),
                column_sum(value_grad[here, :].astype(F32)),
                column_sum(low.astype(F32)),
            ],
        )
        width = 512
        back = jnp.zeros_like(g1)
        for part in range(slope.shape[1] // width):
            cut = slice(part * width, (part + 1) * width)
            inner = (nt(low, reducer[cut, :]) * slope[:, cut].astype(F32)).astype(LOW)
            all_inner[here, cut] = inner
            wide_sums[part : part + 1, :] += column_sum(inner.astype(F32))
            back = back + nt(inner, expand[:, cut])
        unit, scale = normalize(x[...].astype(F32))
        gather_rows(sums, 5, [column_sum(back * unit), column_sum(back)])
        g0 = g1 + norm_backward(back, row_of(table, GAIN_ONE), unit, scale)
        input_gradient[...] = g0.astype(LOW)

    @pl.when(step >= tiles)
    def _():
        grad_reduce[...] = tn(acted[...], all_half[...])
        grad_expand[...] = tn(normed[...], all_inner[...])
        grad_query[...] = tn(normed_b[...], query_grad[...])
        grad_key[...] = tn(normed_b[...], key_grad[...])
        grad_value[...] = tn(normed_b[...], value_grad[...])


def whole(array):
    return pl.BlockSpec(array.shape, lambda step: (0,) * len(array.shape))


def tiled(array):
    if len(array.shape) == 3:
        return pl.BlockSpec((array.shape[0], TILE, array.shape[2]), lambda step: (0, step, 0))
    return pl.BlockSpec((TILE, array.shape[1]), lambda step: (step, 0))


def early(array):
    last = array.shape[-2] // TILE - 1
    if len(array.shape) == 3:
        return pl.BlockSpec((array.shape[0], TILE, array.shape[2]), lambda step: (0, jnp.minimum(step, last), 0))
    return pl.BlockSpec((TILE, array.shape[1]), lambda step: (jnp.minimum(step, last), 0))


def late(skipped):
    def spec(array):
        if len(array.shape) == 3:
            return pl.BlockSpec(
                (array.shape[0], TILE, array.shape[2]), lambda step: (0, jnp.maximum(step - skipped, 0), 0)
            )
        return pl.BlockSpec((TILE, array.shape[1]), lambda step: (jnp.maximum(step - skipped, 0), 0))

    return spec


def row_parts(skipped, parts):
    def spec(array):
        return pl.BlockSpec(
            (array.shape[0] // parts, array.shape[1]), lambda step: (jnp.maximum(step - skipped, 0), 0)
        )

    return spec


def column_parts(skipped, parts):
    def spec(array):
        return pl.BlockSpec(
            (array.shape[0], array.shape[1] // parts), lambda step: (0, jnp.maximum(step - skipped, 0))
        )

    return spec


SCALAR = pl.BlockSpec(memory_space=pltpu.SMEM)


def shaped(dims, dtype):
    return jax.ShapeDtypeStruct(dims, dtype)


def call(kernel, steps, operands, results, scratch=(), flops=0, limit=56, after=()):
    arrays = [array for array, spec in operands]
    moved = sum(array.size * array.dtype.itemsize for array in arrays)
    moved += sum(array.size * array.dtype.itemsize for array, spec in results)
    if after:
        inner = kernel
        start, stop = len(operands), len(operands) + len(after)
        operands = operands + [(array, pl.BlockSpec(memory_space=pl.ANY)) for array in after]
        arrays = arrays + list(after)

        def kernel(*refs):
            inner(*refs[:start], *refs[stop:])

    return pl.pallas_call(
        kernel,
        grid=(steps,),
        in_specs=[spec if isinstance(spec, pl.BlockSpec) else spec(array) for array, spec in operands],
        out_specs=[spec if isinstance(spec, pl.BlockSpec) else spec(array) for array, spec in results],
        out_shape=[array for array, spec in results],
        scratch_shapes=list(scratch),
        compiler_params=pltpu.CompilerParams(vmem_limit_bytes=limit << 20),
        cost_estimate=pl.CostEstimate(flops=flops, bytes_accessed=moved, transcendentals=0),
    )(*arrays)


def bits_of(axis):
    return lax.axis_size(axis).bit_length() - 1


def exchange(values, axis, bit):
    count = lax.axis_size(axis)
    return lax.ppermute(values, axis, [(at, at ^ (1 << bit)) for at in range(count)])


def own_bit(axis, bit):
    return (lax.axis_index(axis) >> bit) & 1


def every_bit():
    return [(axis, bit) for axis in AXES for bit in range(bits_of(axis))]


def sending(values, axis, bit):
    half = values.shape[0] // 2
    return lax.dynamic_slice_in_dim(values, (1 - own_bit(axis, bit)) * half, half)


def keeping(values, axis, bit):
    half = values.shape[0] // 2
    return lax.dynamic_slice_in_dim(values, own_bit(axis, bit) * half, half)


def merged(values, arrived, axis, bit):
    upper = own_bit(axis, bit) == 1
    return jnp.concatenate([jnp.where(upper, arrived, values), jnp.where(upper, values, arrived)])


def part_orders():
    pair = every_bit()[0]
    rest_dp = [step for step in every_bit()[1:] if step[0] == "dp"]
    rest_stream = [step for step in every_bit() if step[0] == "stream"]
    return [
        [pair] + rest_dp + rest_stream,
        [pair] + rest_dp[::-1] + rest_stream,
        [pair] + rest_stream + rest_dp,
    ]


def reduce_kernel(slots, tops):
    count = len(slots)

    def kernel(bits, *refs):
        for at, (slot, top) in enumerate(zip(slots, tops)):
            kept, arrived = refs[2 * at], refs[2 * at + 1]
            rows = arrived.shape[0]
            base = 0 if top is None else pl.multiple_of(bits[top] * rows, 8)
            if slot is None:
                refs[2 * count + at][...] = kept[pl.ds(base, rows), :] + arrived[...]
                continue
            half = rows // 2
            for out, bit in ((2 * count + 2 * at, 1 - bits[slot]), (2 * count + 2 * at + 1, bits[slot])):
                start = pl.multiple_of(bit * half, 8)
                refs[out][...] = kept[pl.ds(base + start, half), :] + arrived[pl.ds(start, half), :]

    return kernel


def split_kernel(slots):
    def kernel(bits, *refs):
        count = len(slots)
        copies = []
        for at, slot in enumerate(slots):
            whole_part, half_part = refs[at], refs[count + at]
            rows = half_part.shape[0]
            start = pl.multiple_of((1 - bits[slot]) * rows, 8)
            copies.append(
                pltpu.make_async_copy(whole_part.at[pl.ds(start, rows), :], half_part, refs[2 * count].at[at])
            )
        for copy in copies:
            copy.start()
        for copy in copies:
            copy.wait()

    return kernel


def gather_kernel(slots):
    count = len(slots)

    def kernel(bits, *refs):
        for at, slot in enumerate(slots):
            mine, arrived, out = refs[2 * at], refs[2 * at + 1], refs[2 * count + at]
            rows = mine.shape[0]
            out[pl.ds(pl.multiple_of(bits[slot] * rows, 8), rows), :] = mine[...]
            out[pl.ds(pl.multiple_of((1 - bits[slot]) * rows, 8), rows), :] = arrived[...]

    return kernel


def one_block(array):
    return pl.BlockSpec(array.shape, lambda step: (0, 0))


class Group:
    def __init__(self, bits, parts, orders, split=False):
        self.bits = bits
        self.orders = [part_orders()[which] for which in orders]
        self.kept = parts
        if split:
            self.sends = call(
                split_kernel(self.slots(0)),
                1,
                [(bits, SCALAR)] + [(part, pl.BlockSpec(memory_space=pl.ANY)) for part in parts],
                [(shaped((part.shape[0] // 2, part.shape[1]), F32), one_block) for part in parts],
                scratch=[pltpu.SemaphoreType.DMA((len(parts),))],
                flops=STAGE_FLOPS,
                limit=STAGE_LIMIT,
            )
        else:
            self.sends = [sending(part, *order[0]) for part, order in zip(parts, self.orders)]
        self.steps = len(self.orders[0])

    def slots(self, at):
        return [every_bit().index(order[at]) for order in self.orders]

    def run(self, kernel, operands, results):
        return call(
            kernel,
            1,
            [(self.bits, SCALAR)] + [(array, one_block) for array in operands],
            [(shaped(dims, F32), one_block) for dims in results],
            flops=STAGE_FLOPS,
            limit=STAGE_LIMIT,
        )

    def reduce(self, at):
        arrived = [exchange(send, *order[at]) for send, order in zip(self.sends, self.orders)]
        tops = self.slots(0) if at == 0 else [None] * len(arrived)
        last = at == self.steps - 1
        slots = [None] * len(arrived) if last else self.slots(at + 1)
        pairs = [array for pair in zip(self.kept, arrived) for array in pair]
        if last:
            self.kept = self.run(reduce_kernel(slots, tops), pairs, [array.shape for array in arrived])
            return
        halves = [(array.shape[0] // 2, array.shape[1]) for array in arrived for twice in range(2)]
        if any(dims[0] % 8 for dims in halves):
            sums = [
                (kept if top is None else keeping(kept, *order[0])) + got
                for kept, got, top, order in zip(self.kept, arrived, tops, self.orders)
            ]
            self.sends = [sending(total, *order[at + 1]) for total, order in zip(sums, self.orders)]
            self.kept = [keeping(total, *order[at + 1]) for total, order in zip(sums, self.orders)]
            return
        found = self.run(reduce_kernel(slots, tops), pairs, halves)
        self.sends, self.kept = found[0::2], found[1::2]

    def gather(self, at):
        arrived = [exchange(mine, *order[at]) for mine, order in zip(self.kept, self.orders)]
        if any(array.shape[0] % 8 for array in arrived):
            self.kept = [
                merged(mine, got, *order[at]) for mine, got, order in zip(self.kept, arrived, self.orders)
            ]
            return
        pairs = [array for pair in zip(self.kept, arrived) for array in pair]
        doubled = [(2 * array.shape[0], array.shape[1]) for array in arrived]
        self.kept = self.run(gather_kernel(self.slots(at)), pairs, doubled)


def sum_groups(groups):
    steps = groups[0].steps
    for at in range(steps):
        for group in groups:
            group.reduce(at)
    for at in reversed(range(steps)):
        for group in groups:
            group.gather(at)
    return [group.kept for group in groups]


def sum_small(values):
    for axis, bit in every_bit():
        values = values + exchange(values, axis, bit)
    return values


def join_moments(packed):
    for axis, bit in every_bit():
        other = exchange(packed, axis, bit)
        both = packed + other
        gap = packed[1] / packed[0] - other[1] / other[0]
        extra = gap * gap * (packed[0] * other[0] / both[0])
        packed = jnp.concatenate([both[0:2], both[2:3] + extra[None], both[3:]])
    return packed


def body(
    inputs, lengths, cotangent,
    gain_one, shift_one, expand_one, lift_one, reduce_one, offset_one,
    attend_gain, attend_shift, query_proj, query_bias, key_proj, value_proj, value_bias, output_proj, output_bias,
    mixing_gain, mixing_shift, point_first, first_bias, depth_kernel, batch_gain, batch_shift, point_second, second_bias,
    gain_two, shift_two, expand_two, lift_two, reduce_two, offset_two, final_gain, final_shift,
):
    utterances, frames, width = inputs.shape
    hidden = expand_one.shape[1]
    steps = frames // TILE
    x = inputs.reshape(frames, width)
    cotangent_rows = cotangent.reshape(frames, width)
    vectors = [
        gain_one, shift_one, offset_one, attend_gain, attend_shift, query_bias, value_bias, output_bias,
        mixing_gain, mixing_shift, batch_gain, batch_shift, second_bias, gain_two, shift_two, offset_two,
        final_gain, final_shift, first_bias, depth_kernel, lift_one, lift_two,
    ]
    table, lift_first, lift_second = call(
        table_kernel,
        1,
        [(vector, whole) for vector in vectors],
        [(shaped(dims, F32), whole) for dims in ((32, width), (1, hidden), (1, hidden))],
        limit=60,
    )
    rows_low = shaped((frames, width), LOW)
    rows_full = shaped((frames, width), F32)
    hidden_low = shaped((frames, hidden), LOW)
    heads_low = shaped((HEADS, frames, LANES), LOW)

    def small(rows):
        return (shaped((rows, width), F32), whole)

    behind = late(steps)
    (
        normed_a, acted_a, slope_a, x1, normed_b, keys, values,
        again, mixed_wide, mixed, x2, normed_c, gated, gate_c, convolved, moments, sums_a,
    ) = call(
        forward_kernel,
        2 * steps,
        [
            (lengths, SCALAR), (x, early), (table, whole), (lift_first, whole), (expand_one, whole),
            (reduce_one, whole), (query_proj, whole), (key_proj, whole), (value_proj, whole),
            (output_proj, whole), (point_first, whole),
        ],
        [
            (rows_low, early), (hidden_low, early), (hidden_low, early), (rows_full, early), (rows_low, early),
            (heads_low, early), (heads_low, early),
            (heads_low, behind), (rows_full, behind), (rows_low, behind), (rows_full, behind), (rows_low, behind),
            (rows_full, behind), (rows_full, behind), (rows_full, whole), small(8), small(8),
        ],
        scratch=[
            pltpu.VMEM((HEADS, frames, LANES), LOW),
            pltpu.VMEM((HEADS, frames, LANES), LOW),
            pltpu.VMEM((HEADS, frames, LANES), LOW),
            pltpu.VMEM((frames, width), F32),
            pltpu.VMEM((frames + 16, width), F32),
        ],
        flops=2 * frames * width * (2 * hidden + 3 * width) + 8 * frames * frames * width,
    )
    moments = join_moments(moments)
    (
        block_output, g3, direct, grad_reduce_two, grad_expand_two, grad_second, sums_c, lift_two_sums,
    ) = call(
        rear_kernel,
        steps + 4,
        [
            (lengths, SCALAR), (convolved, early), (x2, early), (cotangent_rows, early), (moments, whole),
            (table, whole), (lift_second, whole), (point_second, whole), (expand_two, whole), (reduce_two, whole),
        ],
        [
            (rows_low, early), (rows_full, early), (rows_full, early),
            (shaped((hidden, width), F32), row_parts(steps, 4)), (shaped((width, hidden), F32), row_parts(steps, 4)),
            (shaped((width, width), F32), row_parts(steps, 4)), small(16), small(8),
        ],
        scratch=[
            pltpu.VMEM((frames, width), LOW),
            pltpu.VMEM((frames, width), LOW),
            pltpu.VMEM((frames, hidden), LOW),
            pltpu.VMEM((frames, width), LOW),
            pltpu.VMEM((frames, width), LOW),
            pltpu.VMEM((frames, hidden), LOW),
        ],
        flops=2 * frames * width * (6 * hidden + 3 * width),
    )
    batch_sums = sum_small(sums_c[0:8])
    second_large = lax.psum((grad_expand_two, grad_reduce_two), AXES)
    g2, mixed_grads, grad_point_first, grad_output, sums_d = call(
        mixing_kernel,
        steps + 2,
        [
            (lengths, SCALAR), (moments, whole), (batch_sums, whole), (direct, whole), (convolved, whole),
            (gated, early), (gate_c, early), (x2, early), (g3, early), (mixed_wide, early), (table, whole),
            (point_first, whole), (output_proj, whole), (normed_c, column_parts(steps, 2)), (mixed, column_parts(steps, 2)),
        ],
        [
            (rows_full, early), (heads_low, early), (shaped((width, 2 * width), F32), row_parts(steps, 2)),
            (shaped((width, width), F32), row_parts(steps, 2)), small(16),
        ],
        scratch=[
            pltpu.VMEM((frames + 16, width), F32),
            pltpu.VMEM((frames, 2 * width), LOW),
            pltpu.VMEM((frames, width), LOW),
        ],
        flops=2 * frames * width * 6 * width,
    )
    pair_block = pl.BlockSpec((2, frames, LANES), lambda step: (step, 0, 0))
    lane_block = pl.BlockSpec((frames, LANES), lambda step: (0, step))
    query_grad, key_grad, value_grad = call(
        attend_back_kernel,
        HEADS // 2,
        [(again, pair_block), (keys, pair_block), (values, pair_block), (mixed_grads, pair_block)],
        [(rows_low, lane_block), (rows_low, lane_block), (rows_low, lane_block)],
        flops=20 * frames * frames * width,
    )
    parts = row_parts(steps, 4)
    (
        input_gradient, grad_reduce_one, grad_expand_one, grad_query, grad_key, grad_value, sums_e, lift_one_sums,
    ) = call(
        first_back_kernel,
        steps + 4,
        [
            (query_grad, whole), (key_grad, whole), (value_grad, whole), (x1, early), (g2, early), (slope_a, early),
            (table, whole), (query_proj, whole), (key_proj, whole), (value_proj, whole), (reduce_one, whole),
            (acted_a, column_parts(steps, 4)), (normed_a, column_parts(steps, 4)), (normed_b, column_parts(steps, 4)),
            (x, early), (expand_one, whole),
        ],
        [
            (rows_low, early), (shaped((hidden, width), F32), parts),
            (shaped((width, hidden), F32), parts), (shaped((width, width), F32), parts),
            (shaped((width, width), F32), parts), (shaped((width, width), F32), parts), small(8), small(8),
        ],
        scratch=[pltpu.VMEM((frames, width), LOW), pltpu.VMEM((frames, hidden), LOW)],
        flops=2 * frames * width * (3 * hidden + 6 * width),
    )
    bits = jnp.stack([own_bit(axis, bit) for axis, bit in every_bit()]).astype(jnp.int32)
    small_rows = jnp.concatenate(
        [sums_a, sums_c, lift_two_sums, sums_d, sums_e, lift_one_sums, jnp.zeros((192, width), F32)]
    )
    groups = [
        Group(bits, [grad_reduce_one, grad_expand_one], (0, 1), split=True),
        Group(
            bits,
            [
                grad_point_first,
                jnp.concatenate([grad_second, grad_output]),
                jnp.concatenate([grad_query, grad_key, grad_value, small_rows]),
            ],
            (0, 1, 2),
        ),
    ]
    (first_reduce, first_expand), (sum_point_first, sum_square, third) = sum_groups(groups)
    tail = third[3 * width :]
    total_a, total_c, total_lift, total_d, total_e, total_lift_one = (
        tail[0:8], tail[8:24], tail[24:32], tail[32:48], tail[48:56], tail[56:64],
    )
    squares = jnp.sum(
        jnp.stack(
            [
                total_a[0], total_a[2], total_c[8], total_c[10], total_a[1], total_a[3], total_c[9], total_c[11],
            ]
        ),
        axis=1,
    )
    rms_stats = jnp.sqrt(squares / (moments[0, 0] * width))

    return (
        block_output.reshape(inputs.shape),
        input_gradient.reshape(inputs.shape),
        total_e[5],
        total_e[6],
        first_expand,
        total_lift_one[0 : hidden // width].reshape(-1),
        first_reduce,
        total_e[4],
        total_e[0],
        total_e[1],
        third[:width],
        total_e[2],
        third[width : 2 * width],
        third[2 * width : 3 * width],
        total_e[3],
        sum_square[width:],
        total_d[13],
        total_d[0],
        total_d[1],
        sum_point_first,
        total_d[2:4].reshape(-1),
        total_d[4:13],
        batch_sums[1],
        batch_sums[0],
        sum_square[:width],
        total_c[2],
        total_c[3],
        total_c[4],
        second_large[0],
        total_lift[0 : hidden // width].reshape(-1),
        second_large[1],
        total_c[5],
        total_c[6],
        total_c[7],
        rms_stats,
    )


def solution(mesh):
    rows = P(AXES, None, None)
    return jax.shard_map(
        body,
        mesh=mesh,
        in_specs=(rows, P(AXES), rows) + (P(),) * 32,
        out_specs=(rows, rows) + (P(),) * 33,
        check_vma=False,
    )
```

```python
import jax
import jax.numpy as jnp
from jax import lax
from jax.experimental import pallas as pl
from jax.experimental.pallas import tpu as pltpu
from jax.sharding import PartitionSpec as P

HEADS = 8
HEAD = 64
LANES = 128
TILE = 512
EPSILON = 1e-05
AXES = ("dp", "stream")
STAGE_FLOPS = 100_000_000_000
STAGE_LIMIT = 24
F32 = jnp.float32
LOW = jnp.bfloat16

(
    GAIN_ONE,
    SHIFT_ONE,
    OFFSET_ONE,
    ATTEND_GAIN,
    ATTEND_SHIFT,
    QUERY_BIAS,
    VALUE_BIAS,
    OUTPUT_BIAS,
    MIXING_GAIN,
    MIXING_SHIFT,
    BATCH_GAIN,
    BATCH_SHIFT,
    SECOND_BIAS,
    GAIN_TWO,
    SHIFT_TWO,
    OFFSET_TWO,
    FINAL_GAIN,
    FINAL_SHIFT,
    FIRST_BIAS,
) = range(19)
TAPS = 20


def nn(a, b):
    return lax.dot_general(a, b, (((1,), (0,)), ((), ())), preferred_element_type=F32)


def nt(a, b):
    return lax.dot_general(a, b, (((1,), (1,)), ((), ())), preferred_element_type=F32)


def tn(a, b):
    return lax.dot_general(a, b, (((0,), (0,)), ((), ())), preferred_element_type=F32)


def column_sum(values):
    return jnp.sum(values, axis=0, keepdims=True)


def sigmoid(values):
    return 0.5 * jnp.tanh(0.5 * values) + 0.5


def normalize(values):
    centred = values - jnp.mean(values, axis=-1, keepdims=True)
    spread = jnp.mean(centred * centred, axis=-1, keepdims=True)
    scale = lax.rsqrt(spread + EPSILON)
    return centred * scale, scale


def norm_backward(grad, gain, unit, scale):
    inner = grad * gain
    middle = jnp.mean(inner, axis=-1, keepdims=True)
    tilt = jnp.mean(inner * unit, axis=-1, keepdims=True)
    return scale * (inner - middle - unit * tilt)


def row_of(table, at, count=1):
    return table[at : at + count, :]


def valid_rows(lengths_ref, step, rows):
    at = lax.broadcasted_iota(jnp.int32, (rows, 1), 0) + step * rows
    return (at < lengths_ref[0]).astype(F32)


def split_three(values):
    high = values.astype(LOW).astype(F32)
    rest = values - high
    middle = rest.astype(LOW).astype(F32)
    return high, middle, rest - middle


def gather_rows(ref, at, rows):
    for offset, row in enumerate(rows):
        ref[at + offset : at + offset + 1, :] += row


def lane_index(rows):
    return lax.broadcasted_iota(jnp.int32, (rows, LANES), 1)


def head_lanes(values, head):
    pair = values[:, (head // 2) * LANES : (head // 2 + 1) * LANES]
    if head % 2 == 1:
        pair = pltpu.roll(pair, HEAD, 1)
    return pair


def join_pair(even, odd):
    lanes = lane_index(even.shape[0])
    return jnp.where(lanes < HEAD, even, pltpu.roll(odd, HEAD, 1))


def table_kernel(*refs):
    table, lift_first, lift_second = refs[-3:]
    width = table.shape[1]
    for at in range(FIRST_BIAS):
        table[at : at + 1, :] = refs[at][...].astype(F32).reshape(1, width)
    table[FIRST_BIAS : FIRST_BIAS + 2, :] = refs[FIRST_BIAS][...].astype(F32).reshape(2, width)
    table[TAPS : TAPS + 9, :] = refs[FIRST_BIAS + 1][...].astype(F32)
    table[TAPS + 9 :, :] = jnp.zeros((table.shape[0] - TAPS - 9, width), F32)
    lift_first[...] = refs[FIRST_BIAS + 2][...].astype(F32).reshape(lift_first.shape)
    lift_second[...] = refs[FIRST_BIAS + 3][...].astype(F32).reshape(lift_second.shape)


def forward_kernel(
    lengths, x, table, lift, expand, reducer, query, key, value, output, point,
    normed_a, acted, slope, x1, normed_b, keys, values,
    again, mixed_wide, mixed, x2, normed_c, gated, gate_out, convolved, moments, sums,
    all_queries, all_keys, all_values, stream, padded,
):
    step = pl.program_id(0)
    rows = x.shape[0]
    width = x.shape[1]
    tiles = stream.shape[0] // rows

    @pl.when(step == 0)
    def _():
        sums[...] = jnp.zeros_like(sums)
        padded[0:8, :] = jnp.zeros((8, width), F32)
        padded[padded.shape[0] - 8 :, :] = jnp.zeros((8, width), F32)

    lanes = lane_index(rows)

    @pl.when(step < tiles)
    def _():
        valid = valid_rows(lengths, step, rows)
        here = pl.ds(pl.multiple_of(step * rows, rows), rows)
        x0 = x[...].astype(F32)
        unit, scale = normalize(x0)
        low = (unit * row_of(table, GAIN_ONE) + row_of(table, SHIFT_ONE)).astype(LOW)
        normed_a[...] = low
        part_width = 512
        branch = jnp.zeros((rows, width), F32)
        for part in range(expand.shape[1] // part_width):
            cut = slice(part * part_width, (part + 1) * part_width)
            inner = nn(low, expand[:, cut]) + lift[:, cut]
            gate = sigmoid(inner)
            silu = inner * gate
            active = silu.astype(LOW)
            acted[:, cut] = active
            slope[:, cut] = (gate + silu * (1.0 - gate)).astype(LOW)
            branch = branch + nn(active, reducer[cut, :])
        branch = 0.5 * (branch + row_of(table, OFFSET_ONE))
        after = x0 + branch
        x1[...] = after
        stream[here, :] = after
        gather_rows(sums, 0, [column_sum(valid * after * after), column_sum(valid * branch * branch)])
        unit, scale = normalize(after)
        low = (unit * row_of(table, ATTEND_GAIN) + row_of(table, ATTEND_SHIFT)).astype(LOW)
        normed_b[...] = low
        q_all = (nn(low, query[...]) + row_of(table, QUERY_BIAS)).astype(LOW).astype(F32) * HEAD ** (-0.5)
        k_all = nn(low, key[...])
        v_all = nn(low, value[...]) + row_of(table, VALUE_BIAS)
        ones = jnp.where((lanes >= HEAD) & (lanes < HEAD + 4), 1.0, 0.0)
        first = jnp.where(lanes == HEAD, 1.0, 0.0)
        shade = jnp.where(lanes == HEAD, (valid - 1.0) * 1e30, ones)
        for head in range(HEADS):
            all_queries[head, here, :] = jnp.where(lanes < HEAD, head_lanes(q_all, head), first).astype(LOW)
            marked = jnp.where(lanes < HEAD, head_lanes(k_all, head), shade).astype(LOW)
            keys[head, :, :] = marked
            all_keys[head, here, :] = marked
            marked = jnp.where(lanes < HEAD, head_lanes(v_all, head), ones).astype(LOW)
            values[head, :, :] = marked
            all_values[head, here, :] = marked

    @pl.when(step >= tiles)
    def _():
        tile = step - tiles
        valid = valid_rows(lengths, tile, rows)
        here = pl.ds(pl.multiple_of(tile * rows, rows), rows)
        found = []
        for head in range(HEADS):
            query = all_queries[head, here, :]
            scores = nt(query, all_keys[head, :, :])
            top = jnp.max(scores, axis=-1, keepdims=True)
            raised = jnp.exp(scores - top).astype(LOW)
            blend = nn(raised, all_values[head, :, :])
            total = blend[:, HEAD : HEAD + 1]
            found.append(blend * (1.0 / total))
            high, middle, rest = split_three(-(top + jnp.log(total)))
            marked = jnp.where(lanes == HEAD + 1, high, query.astype(F32))
            marked = jnp.where(lanes == HEAD + 2, middle, marked)
            again[head, :, :] = jnp.where(lanes == HEAD + 3, rest, marked).astype(LOW)
        wide = jnp.concatenate(
            [join_pair(found[2 * pair], found[2 * pair + 1]) for pair in range(HEADS // 2)], axis=1
        )
        mixed_wide[...] = wide
        low = wide.astype(LOW)
        mixed[...] = low
        branch = nn(low, output[...]) + row_of(table, OUTPUT_BIAS)
        after = stream[here, :] + branch
        x2[...] = after
        gather_rows(sums, 2, [column_sum(valid * after * after), column_sum(valid * branch * branch)])
        unit, scale = normalize(after)
        low = (unit * row_of(table, MIXING_GAIN) + row_of(table, MIXING_SHIFT)).astype(LOW)
        normed_c[...] = low
        doubled = nn(low, point[...])
        gate = sigmoid(doubled[:, width:] + row_of(table, FIRST_BIAS + 1))
        passed = (doubled[:, :width] + row_of(table, FIRST_BIAS)) * gate * valid
        gated[...] = passed
        gate_out[...] = gate
        padded[pl.ds(pl.multiple_of(8 + tile * rows, 8), rows), :] = passed

    @pl.when(step == pl.num_programs(0) - 1)
    def _():
        frames = convolved.shape[0]
        chunk = 128
        count = lengths[0].astype(F32)
        summed = jnp.zeros((1, width), F32)
        for part in range(frames // chunk):
            total = jnp.zeros((chunk, width), F32)
            for tap in range(9):
                start = part * chunk + 4 + tap
                total = total + padded[start : start + chunk, :] * row_of(table, TAPS + tap)
            convolved[part * chunk : (part + 1) * chunk, :] = total
            here = lax.broadcasted_iota(jnp.int32, (chunk, 1), 0) + part * chunk < lengths[0]
            summed = summed + column_sum(jnp.where(here, total, 0.0))
        mean = summed / count
        spread = jnp.zeros((1, width), F32)
        for part in range(frames // chunk):
            here = lax.broadcasted_iota(jnp.int32, (chunk, 1), 0) + part * chunk < lengths[0]
            apart = jnp.where(here, convolved[part * chunk : (part + 1) * chunk, :] - mean, 0.0)
            spread = spread + column_sum(apart * apart)
        moments[...] = jnp.zeros_like(moments)
        moments[0:1, :] = jnp.full((1, width), count, F32)
        moments[1:2, :] = summed
        moments[2:3, :] = spread


def rear_kernel(
    lengths, convolved, x2, cotangent, moments, table, lift, second, expand, reducer,
    block_output, stream, direct, grad_reduce, grad_expand, grad_second, sums, wide_sums,
    all_acted_c, all_low_c, all_acted, all_half, all_normed, all_inner,
):
    step = pl.program_id(0)

    @pl.when(step == 0)
    def _():
        sums[...] = jnp.zeros_like(sums)
        wide_sums[...] = jnp.zeros_like(wide_sums)

    rows = x2.shape[0]
    tiles = all_acted.shape[0] // rows

    @pl.when(step < tiles)
    def _():
        here = pl.ds(pl.multiple_of(step * rows, rows), rows)
        valid = valid_rows(lengths, step, rows)
        mean = moments[1:2, :] / moments[0:1, :]
        inverse = lax.rsqrt(moments[2:3, :] / moments[0:1, :] + EPSILON)
        unit_c = (convolved[...] - mean) * inverse
        normal = unit_c * row_of(table, BATCH_GAIN) + row_of(table, BATCH_SHIFT)
        gate = sigmoid(normal)
        silu = normal * gate
        slope_c = gate + silu * (1.0 - gate)
        active_c = silu.astype(LOW)
        all_acted_c[here, :] = active_c
        branch = nn(active_c, second[...]) + row_of(table, SECOND_BIAS)
        x3 = x2[...] + branch
        squares = [column_sum(valid * x3 * x3), column_sum(valid * branch * branch)]
        unit_d, scale_d = normalize(x3)
        low_d = (unit_d * row_of(table, GAIN_TWO) + row_of(table, SHIFT_TWO)).astype(LOW)
        all_normed[here, :] = low_d
        width = 512
        parts = expand.shape[1] // width
        branch = jnp.zeros_like(x3)
        slopes = []
        for part in range(parts):
            cut = slice(part * width, (part + 1) * width)
            inner = nn(low_d, expand[:, cut]) + lift[:, cut]
            gate = sigmoid(inner)
            silu = inner * gate
            active = silu.astype(LOW)
            all_acted[here, cut] = active
            slopes.append((gate + silu * (1.0 - gate)).astype(LOW))
            branch = branch + nn(active, reducer[cut, :])
        branch = 0.5 * (branch + row_of(table, OFFSET_TWO))
        x4 = x3 + branch
        squares += [column_sum(valid * x4 * x4), column_sum(valid * branch * branch)]
        unit, scale = normalize(x4)
        gain = row_of(table, FINAL_GAIN)
        block_output[...] = (valid * (unit * gain + row_of(table, FINAL_SHIFT))).astype(LOW)
        grad = cotangent[...].astype(F32) * valid
        closing = [column_sum(grad * unit), column_sum(grad)]
        g4 = norm_backward(grad, gain, unit, scale)
        low = (0.5 * g4).astype(LOW)
        all_half[here, :] = low
        back = jnp.zeros_like(x3)
        for part in range(parts):
            cut = slice(part * width, (part + 1) * width)
            inner = (nt(low, reducer[cut, :]) * slopes[part].astype(F32)).astype(LOW)
            all_inner[here, cut] = inner
            wide_sums[part : part + 1, :] += column_sum(inner.astype(F32))
            back = back + nt(inner, expand[:, cut])
        second_sums = [column_sum(back * unit_d), column_sum(back), column_sum(low.astype(F32))]
        g3 = g4 + norm_backward(back, row_of(table, GAIN_TWO), unit_d, scale_d)
        stream[...] = g3
        low = g3.astype(LOW)
        all_low_c[here, :] = low
        grad = nt(low, second[...]) * slope_c
        direct[...] = grad * (row_of(table, BATCH_GAIN) * inverse)
        gather_rows(
            sums,
            0,
            [column_sum(grad), column_sum(grad * unit_c), column_sum(low.astype(F32))]
            + second_sums
            + closing
            + squares,
        )

    @pl.when(step >= tiles)
    def _():
        part = step - tiles

        def columns(array, count):
            return array[:, pl.ds(pl.multiple_of(part * count, count), count)]

        grad_reduce[...] = tn(columns(all_acted, grad_reduce.shape[0]), all_half[...])
        grad_expand[...] = tn(columns(all_normed, grad_expand.shape[0]), all_inner[...])
        grad_second[...] = tn(columns(all_acted_c, grad_second.shape[0]), all_low_c[...])


def mixing_kernel(
    lengths, moments, batch_sums, direct, convolved, gated, gate, x2, stream, mixed_wide, table, point, output, normed, mixed,
    stream_out, grads, grad_point, grad_output, sums,
    padded, all_doubled, all_out,
):
    step = pl.program_id(0)
    rows = x2.shape[0]
    width = x2.shape[1]
    frames = direct.shape[0]

    @pl.when(step == 0)
    def _():
        sums[...] = jnp.zeros_like(sums)
        count = moments[0:1, :]
        mean = moments[1:2, :] / count
        inverse = lax.rsqrt(moments[2:3, :] / count + EPSILON)
        weight = row_of(table, BATCH_GAIN) * inverse
        mean_grad = -weight * batch_sums[0:1, :] / count
        var_grad = -(inverse * weight) * batch_sums[1:2, :] / count
        padded[0:8, :] = jnp.zeros((8, width), F32)
        padded[padded.shape[0] - 8 :, :] = jnp.zeros((8, width), F32)
        for part in range(frames // rows):
            cut = slice(part * rows, (part + 1) * rows)
            here = lax.broadcasted_iota(jnp.int32, (rows, 1), 0) + part * rows < lengths[0]
            extra = mean_grad + var_grad * (convolved[cut, :] - mean)
            padded[8 + part * rows : 8 + (part + 1) * rows, :] = direct[cut, :] + jnp.where(here, extra, 0.0)

    tiles = frames // rows

    @pl.when(step < tiles)
    def _():
        here = pl.ds(pl.multiple_of(step * rows, rows), rows)
        valid = valid_rows(lengths, step, rows)
        passed = gated[...]
        base = pl.multiple_of(step * rows, 8)
        grad = jnp.zeros((rows, width), F32)
        window = padded[pl.ds(base, rows + 16), :]
        tap_sums = []
        for tap in range(9):
            shifted = window[12 - tap : 12 - tap + rows, :]
            grad = grad + shifted * row_of(table, TAPS + tap)
            tap_sums.append(column_sum(shifted * passed))
        grad = grad * valid
        opened = gate[...]
        left = (grad * opened).astype(LOW)
        right = (grad * passed * (1.0 - opened)).astype(LOW)
        all_doubled[here, :width] = left
        all_doubled[here, width:] = right
        unit, scale = normalize(x2[...])
        back = nt(left, point[:, :width]) + nt(right, point[:, width:])
        g2 = stream[...] + norm_backward(back, row_of(table, MIXING_GAIN), unit, scale)
        stream_out[...] = g2
        low = g2.astype(LOW)
        all_out[here, :] = low
        gather_rows(
            sums,
            0,
            [
                column_sum(back * unit),
                column_sum(back),
                column_sum(left.astype(F32)),
                column_sum(right.astype(F32)),
            ]
            + tap_sums
            + [column_sum(low.astype(F32))],
        )
        grad_mixed = nt(low, output[...]).astype(LOW).astype(F32)
        product = grad_mixed * mixed_wide[...]
        lanes = lane_index(rows)
        for head in range(HEADS):
            pair = product[:, (head // 2) * LANES : (head // 2 + 1) * LANES]
            mine = (lanes < HEAD) if head % 2 == 0 else (lanes >= HEAD)
            inner = jnp.sum(jnp.where(mine, pair, 0.0), axis=-1, keepdims=True)
            high, middle, rest = split_three(-inner)
            marked = jnp.where(lanes < HEAD, head_lanes(grad_mixed, head), 0.0)
            marked = jnp.where(lanes == HEAD + 1, high, marked)
            marked = jnp.where(lanes == HEAD + 2, middle, marked)
            grads[head, :, :] = jnp.where(lanes == HEAD + 3, rest, marked).astype(LOW)

    @pl.when(step >= tiles)
    def _():
        grad_point[...] = tn(normed[...], all_doubled[...])
        grad_output[...] = tn(mixed[...], all_out[...])


def attend_back_kernel(queries, keys, values, grads, query_grad, key_grad, value_grad):
    frames = queries.shape[1]
    chunk = 256
    turned = []
    for side in range(2):
        query = queries[side, :, :]
        grad = grads[side, :, :]
        total = jnp.zeros((LANES, frames), F32)
        key_parts = []
        value_parts = []
        for part in range(frames // chunk):
            cut = slice(part * chunk, (part + 1) * chunk)
            key = keys[side, cut, :]
            softened = jnp.exp(nt(key, query))
            value_parts.append(nn(softened.astype(LOW), grad))
            low = (softened * nt(values[side, cut, :], grad)).astype(LOW)
            key_parts.append(nn(low, query))
            total = total + tn(key, low)
        turned.append((total[0:HEAD, :], key_parts, value_parts))
    both = jnp.concatenate([turned[0][0], turned[1][0]], axis=0) * HEAD ** (-0.5)
    query_grad[...] = both.T.astype(LOW)
    for part in range(frames // chunk):
        cut = slice(part * chunk, (part + 1) * chunk)
        key_grad[cut, :] = join_pair(turned[0][1][part], turned[1][1][part]).astype(LOW)
        value_grad[cut, :] = join_pair(turned[0][2][part], turned[1][2][part]).astype(LOW)


def first_back_kernel(
    query_grad, key_grad, value_grad, x1, stream, slope, table, query, key, value, reducer, acted, normed, normed_b, x, expand,
    input_gradient, grad_reduce, grad_expand, grad_query, grad_key, grad_value, sums, wide_sums,
    all_half, all_inner,
):
    step = pl.program_id(0)

    @pl.when(step == 0)
    def _():
        sums[...] = jnp.zeros_like(sums)
        wide_sums[...] = jnp.zeros_like(wide_sums)

    rows = x1.shape[0]
    tiles = all_half.shape[0] // rows

    @pl.when(step < tiles)
    def _():
        here = pl.ds(pl.multiple_of(step * rows, rows), rows)
        unit, scale = normalize(x1[...])
        back = nt(query_grad[here, :], query[...]) + nt(key_grad[here, :], key[...]) + nt(value_grad[here, :], value[...])
        g1 = stream[...] + norm_backward(back, row_of(table, ATTEND_GAIN), unit, scale)
        low = (0.5 * g1).astype(LOW)
        all_half[here, :] = low
        gather_rows(
            sums,
            0,
            [
                column_sum(back * unit),
                column_sum(back),
                column_sum(query_grad[here, :].astype(F32)),
                column_sum(value_grad[here, :].astype(F32)),
                column_sum(low.astype(F32)),
            ],
        )
        width = 512
        back = jnp.zeros_like(g1)
        for part in range(slope.shape[1] // width):
            cut = slice(part * width, (part + 1) * width)
            inner = (nt(low, reducer[cut, :]) * slope[:, cut].astype(F32)).astype(LOW)
            all_inner[here, cut] = inner
            wide_sums[part : part + 1, :] += column_sum(inner.astype(F32))
            back = back + nt(inner, expand[:, cut])
        unit, scale = normalize(x[...].astype(F32))
        gather_rows(sums, 5, [column_sum(back * unit), column_sum(back)])
        g0 = g1 + norm_backward(back, row_of(table, GAIN_ONE), unit, scale)
        input_gradient[...] = g0.astype(LOW)

    @pl.when(step >= tiles)
    def _():
        grad_reduce[...] = tn(acted[...], all_half[...])
        grad_expand[...] = tn(normed[...], all_inner[...])
        grad_query[...] = tn(normed_b[...], query_grad[...])
        grad_key[...] = tn(normed_b[...], key_grad[...])
        grad_value[...] = tn(normed_b[...], value_grad[...])


def whole(array):
    return pl.BlockSpec(array.shape, lambda step: (0,) * len(array.shape))


def tiled(array):
    if len(array.shape) == 3:
        return pl.BlockSpec((array.shape[0], TILE, array.shape[2]), lambda step: (0, step, 0))
    return pl.BlockSpec((TILE, array.shape[1]), lambda step: (step, 0))


def early(array):
    last = array.shape[-2] // TILE - 1
    if len(array.shape) == 3:
        return pl.BlockSpec((array.shape[0], TILE, array.shape[2]), lambda step: (0, jnp.minimum(step, last), 0))
    return pl.BlockSpec((TILE, array.shape[1]), lambda step: (jnp.minimum(step, last), 0))


def late(skipped):
    def spec(array):
        if len(array.shape) == 3:
            return pl.BlockSpec(
                (array.shape[0], TILE, array.shape[2]), lambda step: (0, jnp.maximum(step - skipped, 0), 0)
            )
        return pl.BlockSpec((TILE, array.shape[1]), lambda step: (jnp.maximum(step - skipped, 0), 0))

    return spec


def row_parts(skipped, parts):
    def spec(array):
        return pl.BlockSpec(
            (array.shape[0] // parts, array.shape[1]), lambda step: (jnp.maximum(step - skipped, 0), 0)
        )

    return spec


def column_parts(skipped, parts):
    def spec(array):
        return pl.BlockSpec(
            (array.shape[0], array.shape[1] // parts), lambda step: (0, jnp.maximum(step - skipped, 0))
        )

    return spec


SCALAR = pl.BlockSpec(memory_space=pltpu.SMEM)


def shaped(dims, dtype):
    return jax.ShapeDtypeStruct(dims, dtype)


def call(kernel, steps, operands, results, scratch=(), flops=0, limit=56, after=()):
    arrays = [array for array, spec in operands]
    moved = sum(array.size * array.dtype.itemsize for array in arrays)
    moved += sum(array.size * array.dtype.itemsize for array, spec in results)
    if after:
        inner = kernel
        start, stop = len(operands), len(operands) + len(after)
        operands = operands + [(array, pl.BlockSpec(memory_space=pl.ANY)) for array in after]
        arrays = arrays + list(after)

        def kernel(*refs):
            inner(*refs[:start], *refs[stop:])

    return pl.pallas_call(
        kernel,
        grid=(steps,),
        in_specs=[spec if isinstance(spec, pl.BlockSpec) else spec(array) for array, spec in operands],
        out_specs=[spec if isinstance(spec, pl.BlockSpec) else spec(array) for array, spec in results],
        out_shape=[array for array, spec in results],
        scratch_shapes=list(scratch),
        compiler_params=pltpu.CompilerParams(vmem_limit_bytes=limit << 20),
        cost_estimate=pl.CostEstimate(flops=flops, bytes_accessed=moved, transcendentals=0),
    )(*arrays)


def bits_of(axis):
    return lax.axis_size(axis).bit_length() - 1


def exchange(values, axis, bit):
    count = lax.axis_size(axis)
    return lax.ppermute(values, axis, [(at, at ^ (1 << bit)) for at in range(count)])


def own_bit(axis, bit):
    return (lax.axis_index(axis) >> bit) & 1


def every_bit():
    return [(axis, bit) for axis in AXES for bit in range(bits_of(axis))]


def sending(values, axis, bit):
    half = values.shape[0] // 2
    return lax.dynamic_slice_in_dim(values, (1 - own_bit(axis, bit)) * half, half)


def keeping(values, axis, bit):
    half = values.shape[0] // 2
    return lax.dynamic_slice_in_dim(values, own_bit(axis, bit) * half, half)


def merged(values, arrived, axis, bit):
    upper = own_bit(axis, bit) == 1
    return jnp.concatenate([jnp.where(upper, arrived, values), jnp.where(upper, values, arrived)])


def part_orders():
    pair = every_bit()[0]
    rest_dp = [step for step in every_bit()[1:] if step[0] == "dp"]
    rest_stream = [step for step in every_bit() if step[0] == "stream"]
    return [
        [pair] + rest_dp + rest_stream,
        [pair] + rest_dp[::-1] + rest_stream[::-1],
        [pair] + rest_stream + rest_dp,
    ]


def reduce_kernel(slots, tops):
    count = len(slots)

    def kernel(bits, *refs):
        for at, (slot, top) in enumerate(zip(slots, tops)):
            kept, arrived = refs[2 * at], refs[2 * at + 1]
            rows = arrived.shape[0]
            base = 0 if top is None else pl.multiple_of(bits[top] * rows, 8)
            if slot is None:
                refs[2 * count + at][...] = kept[pl.ds(base, rows), :] + arrived[...]
                continue
            half = rows // 2
            for out, bit in ((2 * count + 2 * at, 1 - bits[slot]), (2 * count + 2 * at + 1, bits[slot])):
                start = pl.multiple_of(bit * half, 8)
                refs[out][...] = kept[pl.ds(base + start, half), :] + arrived[pl.ds(start, half), :]

    return kernel


def split_kernel(slots):
    def kernel(bits, *refs):
        count = len(slots)
        copies = []
        for at, slot in enumerate(slots):
            whole_part, half_part = refs[at], refs[count + at]
            rows = half_part.shape[0]
            start = pl.multiple_of((1 - bits[slot]) * rows, 8)
            copies.append(
                pltpu.make_async_copy(whole_part.at[pl.ds(start, rows), :], half_part, refs[2 * count].at[at])
            )
        for copy in copies:
            copy.start()
        for copy in copies:
            copy.wait()

    return kernel


def gather_kernel(slots):
    count = len(slots)

    def kernel(bits, *refs):
        for at, slot in enumerate(slots):
            mine, arrived, out = refs[2 * at], refs[2 * at + 1], refs[2 * count + at]
            rows = mine.shape[0]
            out[pl.ds(pl.multiple_of(bits[slot] * rows, 8), rows), :] = mine[...]
            out[pl.ds(pl.multiple_of((1 - bits[slot]) * rows, 8), rows), :] = arrived[...]

    return kernel


def one_block(array):
    return pl.BlockSpec(array.shape, lambda step: (0, 0))


class Group:
    def __init__(self, bits, parts, orders, split=False):
        self.bits = bits
        self.orders = [part_orders()[which] for which in orders]
        self.kept = parts
        if split:
            self.sends = call(
                split_kernel(self.slots(0)),
                1,
                [(bits, SCALAR)] + [(part, pl.BlockSpec(memory_space=pl.ANY)) for part in parts],
                [(shaped((part.shape[0] // 2, part.shape[1]), F32), one_block) for part in parts],
                scratch=[pltpu.SemaphoreType.DMA((len(parts),))],
                flops=STAGE_FLOPS,
                limit=STAGE_LIMIT,
            )
        else:
            self.sends = [sending(part, *order[0]) for part, order in zip(parts, self.orders)]
        self.steps = len(self.orders[0])

    def slots(self, at):
        return [every_bit().index(order[at]) for order in self.orders]

    def run(self, kernel, operands, results):
        return call(
            kernel,
            1,
            [(self.bits, SCALAR)] + [(array, one_block) for array in operands],
            [(shaped(dims, F32), one_block) for dims in results],
            flops=STAGE_FLOPS,
            limit=STAGE_LIMIT,
        )

    def reduce(self, at):
        arrived = [exchange(send, *order[at]) for send, order in zip(self.sends, self.orders)]
        tops = self.slots(0) if at == 0 else [None] * len(arrived)
        last = at == self.steps - 1
        slots = [None] * len(arrived) if last else self.slots(at + 1)
        pairs = [array for pair in zip(self.kept, arrived) for array in pair]
        if last:
            self.kept = self.run(reduce_kernel(slots, tops), pairs, [array.shape for array in arrived])
            return
        halves = [(array.shape[0] // 2, array.shape[1]) for array in arrived for twice in range(2)]
        if any(dims[0] % 8 for dims in halves):
            sums = [
                (kept if top is None else keeping(kept, *order[0])) + got
                for kept, got, top, order in zip(self.kept, arrived, tops, self.orders)
            ]
            self.sends = [sending(total, *order[at + 1]) for total, order in zip(sums, self.orders)]
            self.kept = [keeping(total, *order[at + 1]) for total, order in zip(sums, self.orders)]
            return
        found = self.run(reduce_kernel(slots, tops), pairs, halves)
        self.sends, self.kept = found[0::2], found[1::2]

    def gather(self, at):
        arrived = [exchange(mine, *order[at]) for mine, order in zip(self.kept, self.orders)]
        if any(array.shape[0] % 8 for array in arrived):
            self.kept = [
                merged(mine, got, *order[at]) for mine, got, order in zip(self.kept, arrived, self.orders)
            ]
            return
        pairs = [array for pair in zip(self.kept, arrived) for array in pair]
        doubled = [(2 * array.shape[0], array.shape[1]) for array in arrived]
        self.kept = self.run(gather_kernel(self.slots(at)), pairs, doubled)


def sum_groups(groups):
    steps = groups[0].steps
    for at in range(steps):
        for group in groups:
            group.reduce(at)
    for at in reversed(range(steps)):
        for group in groups:
            group.gather(at)
    return [group.kept for group in groups]


def sum_small(values):
    for axis, bit in every_bit():
        values = values + exchange(values, axis, bit)
    return values


def join_moments(packed):
    for axis, bit in every_bit():
        other = exchange(packed, axis, bit)
        both = packed + other
        gap = packed[1] / packed[0] - other[1] / other[0]
        extra = gap * gap * (packed[0] * other[0] / both[0])
        packed = jnp.concatenate([both[0:2], both[2:3] + extra[None], both[3:]])
    return packed


def body(
    inputs, lengths, cotangent,
    gain_one, shift_one, expand_one, lift_one, reduce_one, offset_one,
    attend_gain, attend_shift, query_proj, query_bias, key_proj, value_proj, value_bias, output_proj, output_bias,
    mixing_gain, mixing_shift, point_first, first_bias, depth_kernel, batch_gain, batch_shift, point_second, second_bias,
    gain_two, shift_two, expand_two, lift_two, reduce_two, offset_two, final_gain, final_shift,
):
    utterances, frames, width = inputs.shape
    hidden = expand_one.shape[1]
    steps = frames // TILE
    x = inputs.reshape(frames, width)
    cotangent_rows = cotangent.reshape(frames, width)
    vectors = [
        gain_one, shift_one, offset_one, attend_gain, attend_shift, query_bias, value_bias, output_bias,
        mixing_gain, mixing_shift, batch_gain, batch_shift, second_bias, gain_two, shift_two, offset_two,
        final_gain, final_shift, first_bias, depth_kernel, lift_one, lift_two,
    ]
    table, lift_first, lift_second = call(
        table_kernel,
        1,
        [(vector, whole) for vector in vectors],
        [(shaped(dims, F32), whole) for dims in ((32, width), (1, hidden), (1, hidden))],
        limit=60,
    )
    rows_low = shaped((frames, width), LOW)
    rows_full = shaped((frames, width), F32)
    hidden_low = shaped((frames, hidden), LOW)
    heads_low = shaped((HEADS, frames, LANES), LOW)

    def small(rows):
        return (shaped((rows, width), F32), whole)

    behind = late(steps)
    (
        normed_a, acted_a, slope_a, x1, normed_b, keys, values,
        again, mixed_wide, mixed, x2, normed_c, gated, gate_c, convolved, moments, sums_a,
    ) = call(
        forward_kernel,
        2 * steps,
        [
            (lengths, SCALAR), (x, early), (table, whole), (lift_first, whole), (expand_one, whole),
            (reduce_one, whole), (query_proj, whole), (key_proj, whole), (value_proj, whole),
            (output_proj, whole), (point_first, whole),
        ],
        [
            (rows_low, early), (hidden_low, early), (hidden_low, early), (rows_full, early), (rows_low, early),
            (heads_low, early), (heads_low, early),
            (heads_low, behind), (rows_full, behind), (rows_low, behind), (rows_full, behind), (rows_low, behind),
            (rows_full, behind), (rows_full, behind), (rows_full, whole), small(8), small(8),
        ],
        scratch=[
            pltpu.VMEM((HEADS, frames, LANES), LOW),
            pltpu.VMEM((HEADS, frames, LANES), LOW),
            pltpu.VMEM((HEADS, frames, LANES), LOW),
            pltpu.VMEM((frames, width), F32),
            pltpu.VMEM((frames + 16, width), F32),
        ],
        limit=56,
        flops=2 * frames * width * (2 * hidden + 3 * width) + 8 * frames * frames * width,
    )
    moments = join_moments(moments)
    (
        block_output, g3, direct, grad_reduce_two, grad_expand_two, grad_second, sums_c, lift_two_sums,
    ) = call(
        rear_kernel,
        steps + 4,
        [
            (lengths, SCALAR), (convolved, early), (x2, early), (cotangent_rows, early), (moments, whole),
            (table, whole), (lift_second, whole), (point_second, whole), (expand_two, whole), (reduce_two, whole),
        ],
        [
            (rows_low, early), (rows_full, early), (rows_full, early),
            (shaped((hidden, width), F32), row_parts(steps, 4)), (shaped((width, hidden), F32), row_parts(steps, 4)),
            (shaped((width, width), F32), row_parts(steps, 4)), small(16), small(8),
        ],
        scratch=[
            pltpu.VMEM((frames, width), LOW),
            pltpu.VMEM((frames, width), LOW),
            pltpu.VMEM((frames, hidden), LOW),
            pltpu.VMEM((frames, width), LOW),
            pltpu.VMEM((frames, width), LOW),
            pltpu.VMEM((frames, hidden), LOW),
        ],
        limit=56,
        flops=2 * frames * width * (6 * hidden + 3 * width),
    )
    batch_sums = sum_small(sums_c[0:8])
    second_large = lax.psum((grad_expand_two, grad_reduce_two), AXES)
    g2, mixed_grads, grad_point_first, grad_output, sums_d = call(
        mixing_kernel,
        steps + 2,
        [
            (lengths, SCALAR), (moments, whole), (batch_sums, whole), (direct, whole), (convolved, whole),
            (gated, early), (gate_c, early), (x2, early), (g3, early), (mixed_wide, early), (table, whole),
            (point_first, whole), (output_proj, whole), (normed_c, column_parts(steps, 2)), (mixed, column_parts(steps, 2)),
        ],
        [
            (rows_full, early), (heads_low, early), (shaped((width, 2 * width), F32), row_parts(steps, 2)),
            (shaped((width, width), F32), row_parts(steps, 2)), small(16),
        ],
        scratch=[
            pltpu.VMEM((frames + 16, width), F32),
            pltpu.VMEM((frames, 2 * width), LOW),
            pltpu.VMEM((frames, width), LOW),
        ],
        limit=56,
        flops=2 * frames * width * 6 * width,
    )
    pair_block = pl.BlockSpec((2, frames, LANES), lambda step: (step, 0, 0))
    lane_block = pl.BlockSpec((frames, LANES), lambda step: (0, step))
    query_grad, key_grad, value_grad = call(
        attend_back_kernel,
        HEADS // 2,
        [(again, pair_block), (keys, pair_block), (values, pair_block), (mixed_grads, pair_block)],
        [(rows_low, lane_block), (rows_low, lane_block), (rows_low, lane_block)],
        limit=20,
        flops=20 * frames * frames * width,
    )
    parts = row_parts(steps, 4)
    (
        input_gradient, grad_reduce_one, grad_expand_one, grad_query, grad_key, grad_value, sums_e, lift_one_sums,
    ) = call(
        first_back_kernel,
        steps + 4,
        [
            (query_grad, whole), (key_grad, whole), (value_grad, whole), (x1, early), (g2, early), (slope_a, early),
            (table, whole), (query_proj, whole), (key_proj, whole), (value_proj, whole), (reduce_one, whole),
            (acted_a, column_parts(steps, 4)), (normed_a, column_parts(steps, 4)), (normed_b, column_parts(steps, 4)),
            (x, early), (expand_one, whole),
        ],
        [
            (rows_low, early), (shaped((hidden, width), F32), parts),
            (shaped((width, hidden), F32), parts), (shaped((width, width), F32), parts),
            (shaped((width, width), F32), parts), (shaped((width, width), F32), parts), small(8), small(8),
        ],
        scratch=[pltpu.VMEM((frames, width), LOW), pltpu.VMEM((frames, hidden), LOW)],
        limit=44,
        flops=2 * frames * width * (3 * hidden + 6 * width),
    )
    bits = jnp.stack([own_bit(axis, bit) for axis, bit in every_bit()]).astype(jnp.int32)
    small_rows = jnp.concatenate(
        [sums_a, sums_c, lift_two_sums, sums_d, sums_e, lift_one_sums, jnp.zeros((192, width), F32)]
    )
    groups = [
        Group(bits, [grad_reduce_one, grad_expand_one], (0, 1), split=True),
        Group(
            bits,
            [
                grad_point_first,
                jnp.concatenate([grad_second, grad_output]),
                jnp.concatenate([grad_query, grad_key, grad_value, small_rows]),
            ],
            (0, 1, 2),
        ),
    ]
    (first_reduce, first_expand), (sum_point_first, sum_square, third) = sum_groups(groups)
    tail = third[3 * width :]
    total_a, total_c, total_lift, total_d, total_e, total_lift_one = (
        tail[0:8], tail[8:24], tail[24:32], tail[32:48], tail[48:56], tail[56:64],
    )
    squares = jnp.sum(
        jnp.stack(
            [
                total_a[0], total_a[2], total_c[8], total_c[10], total_a[1], total_a[3], total_c[9], total_c[11],
            ]
        ),
        axis=1,
    )
    rms_stats = jnp.sqrt(squares / (moments[0, 0] * width))

    return (
        block_output.reshape(inputs.shape),
        input_gradient.reshape(inputs.shape),
        total_e[5],
        total_e[6],
        first_expand,
        total_lift_one[0 : hidden // width].reshape(-1),
        first_reduce,
        total_e[4],
        total_e[0],
        total_e[1],
        third[:width],
        total_e[2],
        third[width : 2 * width],
        third[2 * width : 3 * width],
        total_e[3],
        sum_square[width:],
        total_d[13],
        total_d[0],
        total_d[1],
        sum_point_first,
        total_d[2:4].reshape(-1),
        total_d[4:13],
        batch_sums[1],
        batch_sums[0],
        sum_square[:width],
        total_c[2],
        total_c[3],
        total_c[4],
        second_large[0],
        total_lift[0 : hidden // width].reshape(-1),
        second_large[1],
        total_c[5],
        total_c[6],
        total_c[7],
        rms_stats,
    )


def solution(mesh):
    rows = P(AXES, None, None)
    return jax.shard_map(
        body,
        mesh=mesh,
        in_specs=(rows, P(AXES), rows) + (P(),) * 32,
        out_specs=(rows, rows) + (P(),) * 33,
        check_vma=False,
    )
```

```python
import jax
import jax.numpy as jnp
from jax import lax
from jax.experimental import pallas as pl
from jax.experimental.pallas import tpu as pltpu
from jax.sharding import PartitionSpec as P

HEADS = 8
HEAD = 64
LANES = 128
TILE = 512
EPSILON = 1e-05
AXES = ("dp", "stream")
STAGE_FLOPS = 100_000_000_000
STAGE_LIMIT = 24
F32 = jnp.float32
LOW = jnp.bfloat16

(
    GAIN_ONE,
    SHIFT_ONE,
    OFFSET_ONE,
    ATTEND_GAIN,
    ATTEND_SHIFT,
    QUERY_BIAS,
    VALUE_BIAS,
    OUTPUT_BIAS,
    MIXING_GAIN,
    MIXING_SHIFT,
    BATCH_GAIN,
    BATCH_SHIFT,
    SECOND_BIAS,
    GAIN_TWO,
    SHIFT_TWO,
    OFFSET_TWO,
    FINAL_GAIN,
    FINAL_SHIFT,
    FIRST_BIAS,
) = range(19)
TAPS = 20


def nn(a, b):
    return lax.dot_general(a, b, (((1,), (0,)), ((), ())), preferred_element_type=F32)


def nt(a, b):
    return lax.dot_general(a, b, (((1,), (1,)), ((), ())), preferred_element_type=F32)


def tn(a, b):
    return lax.dot_general(a, b, (((0,), (0,)), ((), ())), preferred_element_type=F32)


def column_sum(values):
    return jnp.sum(values, axis=0, keepdims=True)


def sigmoid(values):
    return 0.5 * jnp.tanh(0.5 * values) + 0.5


def normalize(values):
    centred = values - jnp.mean(values, axis=-1, keepdims=True)
    spread = jnp.mean(centred * centred, axis=-1, keepdims=True)
    scale = lax.rsqrt(spread + EPSILON)
    return centred * scale, scale


def norm_backward(grad, gain, unit, scale):
    inner = grad * gain
    middle = jnp.mean(inner, axis=-1, keepdims=True)
    tilt = jnp.mean(inner * unit, axis=-1, keepdims=True)
    return scale * (inner - middle - unit * tilt)


def row_of(table, at, count=1):
    return table[at : at + count, :]


def valid_rows(lengths_ref, step, rows):
    at = lax.broadcasted_iota(jnp.int32, (rows, 1), 0) + step * rows
    return (at < lengths_ref[0]).astype(F32)


def split_three(values):
    high = values.astype(LOW).astype(F32)
    rest = values - high
    middle = rest.astype(LOW).astype(F32)
    return high, middle, rest - middle


def gather_rows(ref, at, rows):
    for offset, row in enumerate(rows):
        ref[at + offset : at + offset + 1, :] += row


def lane_index(rows):
    return lax.broadcasted_iota(jnp.int32, (rows, LANES), 1)


def head_lanes(values, head):
    pair = values[:, (head // 2) * LANES : (head // 2 + 1) * LANES]
    if head % 2 == 1:
        pair = pltpu.roll(pair, HEAD, 1)
    return pair


def join_pair(even, odd):
    lanes = lane_index(even.shape[0])
    return jnp.where(lanes < HEAD, even, pltpu.roll(odd, HEAD, 1))


def table_kernel(*refs):
    table, lift_first, lift_second = refs[-3:]
    width = table.shape[1]
    for at in range(FIRST_BIAS):
        table[at : at + 1, :] = refs[at][...].astype(F32).reshape(1, width)
    table[FIRST_BIAS : FIRST_BIAS + 2, :] = refs[FIRST_BIAS][...].astype(F32).reshape(2, width)
    table[TAPS : TAPS + 9, :] = refs[FIRST_BIAS + 1][...].astype(F32)
    table[TAPS + 9 :, :] = jnp.zeros((table.shape[0] - TAPS - 9, width), F32)
    lift_first[...] = refs[FIRST_BIAS + 2][...].astype(F32).reshape(lift_first.shape)
    lift_second[...] = refs[FIRST_BIAS + 3][...].astype(F32).reshape(lift_second.shape)


def forward_kernel(
    lengths, x, table, lift, expand, reducer, query, key, value, output, point,
    normed_a, acted, slope, x1, normed_b, keys, values,
    again, mixed_wide, mixed, x2, normed_c, gated, gate_out, convolved, moments, sums,
    all_queries, all_keys, all_values, stream, padded,
):
    step = pl.program_id(0)
    rows = x.shape[0]
    width = x.shape[1]
    tiles = stream.shape[0] // rows

    @pl.when(step == 0)
    def _():
        sums[...] = jnp.zeros_like(sums)
        padded[0:8, :] = jnp.zeros((8, width), F32)
        padded[padded.shape[0] - 8 :, :] = jnp.zeros((8, width), F32)

    lanes = lane_index(rows)

    @pl.when(step < tiles)
    def _():
        valid = valid_rows(lengths, step, rows)
        here = pl.ds(pl.multiple_of(step * rows, rows), rows)
        x0 = x[...].astype(F32)
        unit, scale = normalize(x0)
        low = (unit * row_of(table, GAIN_ONE) + row_of(table, SHIFT_ONE)).astype(LOW)
        normed_a[...] = low
        part_width = 512
        branch = jnp.zeros((rows, width), F32)
        for part in range(expand.shape[1] // part_width):
            cut = slice(part * part_width, (part + 1) * part_width)
            inner = nn(low, expand[:, cut]) + lift[:, cut]
            gate = sigmoid(inner)
            silu = inner * gate
            active = silu.astype(LOW)
            acted[:, cut] = active
            slope[:, cut] = (gate + silu * (1.0 - gate)).astype(LOW)
            branch = branch + nn(active, reducer[cut, :])
        branch = 0.5 * (branch + row_of(table, OFFSET_ONE))
        after = x0 + branch
        x1[...] = after
        stream[here, :] = after
        gather_rows(sums, 0, [column_sum(valid * after * after), column_sum(valid * branch * branch)])
        unit, scale = normalize(after)
        low = (unit * row_of(table, ATTEND_GAIN) + row_of(table, ATTEND_SHIFT)).astype(LOW)
        normed_b[...] = low
        q_all = (nn(low, query[...]) + row_of(table, QUERY_BIAS)).astype(LOW).astype(F32) * HEAD ** (-0.5)
        k_all = nn(low, key[...])
        v_all = nn(low, value[...]) + row_of(table, VALUE_BIAS)
        ones = jnp.where((lanes >= HEAD) & (lanes < HEAD + 4), 1.0, 0.0)
        first = jnp.where(lanes == HEAD, 1.0, 0.0)
        shade = jnp.where(lanes == HEAD, (valid - 1.0) * 1e30, ones)
        for head in range(HEADS):
            all_queries[head, here, :] = jnp.where(lanes < HEAD, head_lanes(q_all, head), first).astype(LOW)
            marked = jnp.where(lanes < HEAD, head_lanes(k_all, head), shade).astype(LOW)
            keys[head, :, :] = marked
            all_keys[head, here, :] = marked
            marked = jnp.where(lanes < HEAD, head_lanes(v_all, head), ones).astype(LOW)
            values[head, :, :] = marked
            all_values[head, here, :] = marked

    @pl.when(step >= tiles)
    def _():
        tile = step - tiles
        valid = valid_rows(lengths, tile, rows)
        here = pl.ds(pl.multiple_of(tile * rows, rows), rows)
        found = []
        for head in range(HEADS):
            query = all_queries[head, here, :]
            scores = nt(query, all_keys[head, :, :])
            top = jnp.max(scores, axis=-1, keepdims=True)
            raised = jnp.exp(scores - top).astype(LOW)
            blend = nn(raised, all_values[head, :, :])
            total = blend[:, HEAD : HEAD + 1]
            found.append(blend * (1.0 / total))
            high, middle, rest = split_three(-(top + jnp.log(total)))
            marked = jnp.where(lanes == HEAD + 1, high, query.astype(F32))
            marked = jnp.where(lanes == HEAD + 2, middle, marked)
            again[head, :, :] = jnp.where(lanes == HEAD + 3, rest, marked).astype(LOW)
        wide = jnp.concatenate(
            [join_pair(found[2 * pair], found[2 * pair + 1]) for pair in range(HEADS // 2)], axis=1
        )
        mixed_wide[...] = wide
        low = wide.astype(LOW)
        mixed[...] = low
        branch = nn(low, output[...]) + row_of(table, OUTPUT_BIAS)
        after = stream[here, :] + branch
        x2[...] = after
        gather_rows(sums, 2, [column_sum(valid * after * after), column_sum(valid * branch * branch)])
        unit, scale = normalize(after)
        low = (unit * row_of(table, MIXING_GAIN) + row_of(table, MIXING_SHIFT)).astype(LOW)
        normed_c[...] = low
        doubled = nn(low, point[...])
        gate = sigmoid(doubled[:, width:] + row_of(table, FIRST_BIAS + 1))
        passed = (doubled[:, :width] + row_of(table, FIRST_BIAS)) * gate * valid
        gated[...] = passed
        gate_out[...] = gate
        padded[pl.ds(pl.multiple_of(8 + tile * rows, 8), rows), :] = passed

    @pl.when(step == pl.num_programs(0) - 1)
    def _():
        frames = convolved.shape[0]
        chunk = 128
        count = lengths[0].astype(F32)
        summed = jnp.zeros((1, width), F32)
        for part in range(frames // chunk):
            total = jnp.zeros((chunk, width), F32)
            for tap in range(9):
                start = part * chunk + 4 + tap
                total = total + padded[start : start + chunk, :] * row_of(table, TAPS + tap)
            convolved[part * chunk : (part + 1) * chunk, :] = total
            here = lax.broadcasted_iota(jnp.int32, (chunk, 1), 0) + part * chunk < lengths[0]
            summed = summed + column_sum(jnp.where(here, total, 0.0))
        mean = summed / count
        spread = jnp.zeros((1, width), F32)
        for part in range(frames // chunk):
            here = lax.broadcasted_iota(jnp.int32, (chunk, 1), 0) + part * chunk < lengths[0]
            apart = jnp.where(here, convolved[part * chunk : (part + 1) * chunk, :] - mean, 0.0)
            spread = spread + column_sum(apart * apart)
        moments[...] = jnp.zeros_like(moments)
        moments[0:1, :] = jnp.full((1, width), count, F32)
        moments[1:2, :] = summed
        moments[2:3, :] = spread


def rear_kernel(
    lengths, convolved, x2, cotangent, moments, table, lift, second, expand, reducer,
    block_output, stream, direct, grad_reduce, grad_expand, grad_second, sums, wide_sums,
    all_acted_c, all_low_c, all_acted, all_half, all_normed, all_inner,
):
    step = pl.program_id(0)

    @pl.when(step == 0)
    def _():
        sums[...] = jnp.zeros_like(sums)
        wide_sums[...] = jnp.zeros_like(wide_sums)

    rows = x2.shape[0]
    tiles = all_acted.shape[0] // rows

    @pl.when(step < tiles)
    def _():
        here = pl.ds(pl.multiple_of(step * rows, rows), rows)
        valid = valid_rows(lengths, step, rows)
        mean = moments[1:2, :] / moments[0:1, :]
        inverse = lax.rsqrt(moments[2:3, :] / moments[0:1, :] + EPSILON)
        unit_c = (convolved[...] - mean) * inverse
        normal = unit_c * row_of(table, BATCH_GAIN) + row_of(table, BATCH_SHIFT)
        gate = sigmoid(normal)
        silu = normal * gate
        slope_c = gate + silu * (1.0 - gate)
        active_c = silu.astype(LOW)
        all_acted_c[here, :] = active_c
        branch = nn(active_c, second[...]) + row_of(table, SECOND_BIAS)
        x3 = x2[...] + branch
        squares = [column_sum(valid * x3 * x3), column_sum(valid * branch * branch)]
        unit_d, scale_d = normalize(x3)
        low_d = (unit_d * row_of(table, GAIN_TWO) + row_of(table, SHIFT_TWO)).astype(LOW)
        all_normed[here, :] = low_d
        width = 512
        parts = expand.shape[1] // width
        branch = jnp.zeros_like(x3)
        slopes = []
        for part in range(parts):
            cut = slice(part * width, (part + 1) * width)
            inner = nn(low_d, expand[:, cut]) + lift[:, cut]
            gate = sigmoid(inner)
            silu = inner * gate
            active = silu.astype(LOW)
            all_acted[here, cut] = active
            slopes.append((gate + silu * (1.0 - gate)).astype(LOW))
            branch = branch + nn(active, reducer[cut, :])
        branch = 0.5 * (branch + row_of(table, OFFSET_TWO))
        x4 = x3 + branch
        squares += [column_sum(valid * x4 * x4), column_sum(valid * branch * branch)]
        unit, scale = normalize(x4)
        gain = row_of(table, FINAL_GAIN)
        block_output[...] = (valid * (unit * gain + row_of(table, FINAL_SHIFT))).astype(LOW)
        grad = cotangent[...].astype(F32) * valid
        closing = [column_sum(grad * unit), column_sum(grad)]
        g4 = norm_backward(grad, gain, unit, scale)
        low = (0.5 * g4).astype(LOW)
        all_half[here, :] = low
        back = jnp.zeros_like(x3)
        for part in range(parts):
            cut = slice(part * width, (part + 1) * width)
            inner = (nt(low, reducer[cut, :]) * slopes[part].astype(F32)).astype(LOW)
            all_inner[here, cut] = inner
            wide_sums[part : part + 1, :] += column_sum(inner.astype(F32))
            back = back + nt(inner, expand[:, cut])
        second_sums = [column_sum(back * unit_d), column_sum(back), column_sum(low.astype(F32))]
        g3 = g4 + norm_backward(back, row_of(table, GAIN_TWO), unit_d, scale_d)
        stream[...] = g3
        low = g3.astype(LOW)
        all_low_c[here, :] = low
        grad = nt(low, second[...]) * slope_c
        direct[...] = grad * (row_of(table, BATCH_GAIN) * inverse)
        gather_rows(
            sums,
            0,
            [column_sum(grad), column_sum(grad * unit_c), column_sum(low.astype(F32))]
            + second_sums
            + closing
            + squares,
        )

    @pl.when(step >= tiles)
    def _():
        part = step - tiles

        def columns(array, count):
            return array[:, pl.ds(pl.multiple_of(part * count, count), count)]

        grad_reduce[...] = tn(columns(all_acted, grad_reduce.shape[0]), all_half[...])
        grad_expand[...] = tn(columns(all_normed, grad_expand.shape[0]), all_inner[...])
        grad_second[...] = tn(columns(all_acted_c, grad_second.shape[0]), all_low_c[...])


def mixing_kernel(
    lengths, moments, batch_sums, direct, convolved, gated, gate, x2, stream, mixed_wide, table, point, output, normed, mixed,
    stream_out, grads, grad_point, grad_output, sums,
    padded, all_doubled, all_out,
):
    step = pl.program_id(0)
    rows = x2.shape[0]
    width = x2.shape[1]
    frames = direct.shape[0]

    @pl.when(step == 0)
    def _():
        sums[...] = jnp.zeros_like(sums)
        count = moments[0:1, :]
        mean = moments[1:2, :] / count
        inverse = lax.rsqrt(moments[2:3, :] / count + EPSILON)
        weight = row_of(table, BATCH_GAIN) * inverse
        mean_grad = -weight * batch_sums[0:1, :] / count
        var_grad = -(inverse * weight) * batch_sums[1:2, :] / count
        padded[0:8, :] = jnp.zeros((8, width), F32)
        padded[padded.shape[0] - 8 :, :] = jnp.zeros((8, width), F32)
        for part in range(frames // rows):
            cut = slice(part * rows, (part + 1) * rows)
            here = lax.broadcasted_iota(jnp.int32, (rows, 1), 0) + part * rows < lengths[0]
            extra = mean_grad + var_grad * (convolved[cut, :] - mean)
            padded[8 + part * rows : 8 + (part + 1) * rows, :] = direct[cut, :] + jnp.where(here, extra, 0.0)

    tiles = frames // rows

    @pl.when(step < tiles)
    def _():
        here = pl.ds(pl.multiple_of(step * rows, rows), rows)
        valid = valid_rows(lengths, step, rows)
        passed = gated[...]
        base = pl.multiple_of(step * rows, 8)
        grad = jnp.zeros((rows, width), F32)
        window = padded[pl.ds(base, rows + 16), :]
        tap_sums = []
        for tap in range(9):
            shifted = window[12 - tap : 12 - tap + rows, :]
            grad = grad + shifted * row_of(table, TAPS + tap)
            tap_sums.append(column_sum(shifted * passed))
        grad = grad * valid
        opened = gate[...]
        left = (grad * opened).astype(LOW)
        right = (grad * passed * (1.0 - opened)).astype(LOW)
        all_doubled[here, :width] = left
        all_doubled[here, width:] = right
        unit, scale = normalize(x2[...])
        back = nt(left, point[:, :width]) + nt(right, point[:, width:])
        g2 = stream[...] + norm_backward(back, row_of(table, MIXING_GAIN), unit, scale)
        stream_out[...] = g2
        low = g2.astype(LOW)
        all_out[here, :] = low
        gather_rows(
            sums,
            0,
            [
                column_sum(back * unit),
                column_sum(back),
                column_sum(left.astype(F32)),
                column_sum(right.astype(F32)),
            ]
            + tap_sums
            + [column_sum(low.astype(F32))],
        )
        grad_mixed = nt(low, output[...]).astype(LOW).astype(F32)
        product = grad_mixed * mixed_wide[...]
        lanes = lane_index(rows)
        for head in range(HEADS):
            pair = product[:, (head // 2) * LANES : (head // 2 + 1) * LANES]
            mine = (lanes < HEAD) if head % 2 == 0 else (lanes >= HEAD)
            inner = jnp.sum(jnp.where(mine, pair, 0.0), axis=-1, keepdims=True)
            high, middle, rest = split_three(-inner)
            marked = jnp.where(lanes < HEAD, head_lanes(grad_mixed, head), 0.0)
            marked = jnp.where(lanes == HEAD + 1, high, marked)
            marked = jnp.where(lanes == HEAD + 2, middle, marked)
            grads[head, :, :] = jnp.where(lanes == HEAD + 3, rest, marked).astype(LOW)

    @pl.when(step >= tiles)
    def _():
        grad_point[...] = tn(normed[...], all_doubled[...])
        grad_output[...] = tn(mixed[...], all_out[...])


def attend_back_kernel(queries, keys, values, grads, query_grad, key_grad, value_grad):
    frames = queries.shape[1]
    chunk = 256
    turned = []
    for side in range(2):
        query = queries[side, :, :]
        grad = grads[side, :, :]
        total = jnp.zeros((LANES, frames), F32)
        key_parts = []
        value_parts = []
        for part in range(frames // chunk):
            cut = slice(part * chunk, (part + 1) * chunk)
            key = keys[side, cut, :]
            softened = jnp.exp(nt(key, query))
            value_parts.append(nn(softened.astype(LOW), grad))
            low = (softened * nt(values[side, cut, :], grad)).astype(LOW)
            key_parts.append(nn(low, query))
            total = total + tn(key, low)
        turned.append((total[0:HEAD, :], key_parts, value_parts))
    both = jnp.concatenate([turned[0][0], turned[1][0]], axis=0) * HEAD ** (-0.5)
    query_grad[...] = both.T.astype(LOW)
    for part in range(frames // chunk):
        cut = slice(part * chunk, (part + 1) * chunk)
        key_grad[cut, :] = join_pair(turned[0][1][part], turned[1][1][part]).astype(LOW)
        value_grad[cut, :] = join_pair(turned[0][2][part], turned[1][2][part]).astype(LOW)


def first_back_kernel(
    query_grad, key_grad, value_grad, x1, stream, slope, table, query, key, value, reducer, acted, normed, normed_b, x, expand,
    input_gradient, grad_reduce, grad_expand, grad_query, grad_key, grad_value, sums, wide_sums,
    all_half, all_inner,
):
    step = pl.program_id(0)

    @pl.when(step == 0)
    def _():
        sums[...] = jnp.zeros_like(sums)
        wide_sums[...] = jnp.zeros_like(wide_sums)

    rows = x1.shape[0]
    tiles = all_half.shape[0] // rows

    @pl.when(step < tiles)
    def _():
        here = pl.ds(pl.multiple_of(step * rows, rows), rows)
        unit, scale = normalize(x1[...])
        back = nt(query_grad[here, :], query[...]) + nt(key_grad[here, :], key[...]) + nt(value_grad[here, :], value[...])
        g1 = stream[...] + norm_backward(back, row_of(table, ATTEND_GAIN), unit, scale)
        low = (0.5 * g1).astype(LOW)
        all_half[here, :] = low
        gather_rows(
            sums,
            0,
            [
                column_sum(back * unit),
                column_sum(back),
                column_sum(query_grad[here, :].astype(F32)),
                column_sum(value_grad[here, :].astype(F32)),
                column_sum(low.astype(F32)),
            ],
        )
        width = 512
        back = jnp.zeros_like(g1)
        for part in range(slope.shape[1] // width):
            cut = slice(part * width, (part + 1) * width)
            inner = (nt(low, reducer[cut, :]) * slope[:, cut].astype(F32)).astype(LOW)
            all_inner[here, cut] = inner
            wide_sums[part : part + 1, :] += column_sum(inner.astype(F32))
            back = back + nt(inner, expand[:, cut])
        unit, scale = normalize(x[...].astype(F32))
        gather_rows(sums, 5, [column_sum(back * unit), column_sum(back)])
        g0 = g1 + norm_backward(back, row_of(table, GAIN_ONE), unit, scale)
        input_gradient[...] = g0.astype(LOW)

    @pl.when(step >= tiles)
    def _():
        grad_reduce[...] = tn(acted[...], all_half[...])
        grad_expand[...] = tn(normed[...], all_inner[...])
        grad_query[...] = tn(normed_b[...], query_grad[...])
        grad_key[...] = tn(normed_b[...], key_grad[...])
        grad_value[...] = tn(normed_b[...], value_grad[...])


def whole(array):
    return pl.BlockSpec(array.shape, lambda step: (0,) * len(array.shape))


def tiled(array):
    if len(array.shape) == 3:
        return pl.BlockSpec((array.shape[0], TILE, array.shape[2]), lambda step: (0, step, 0))
    return pl.BlockSpec((TILE, array.shape[1]), lambda step: (step, 0))


def early(array, tile=TILE):
    last = array.shape[-2] // tile - 1
    if len(array.shape) == 3:
        return pl.BlockSpec((array.shape[0], tile, array.shape[2]), lambda step: (0, jnp.minimum(step, last), 0))
    return pl.BlockSpec((tile, array.shape[1]), lambda step: (jnp.minimum(step, last), 0))


def early_half(array):
    return early(array, TILE // 2)


def late(skipped):
    def spec(array):
        if len(array.shape) == 3:
            return pl.BlockSpec(
                (array.shape[0], TILE, array.shape[2]), lambda step: (0, jnp.maximum(step - skipped, 0), 0)
            )
        return pl.BlockSpec((TILE, array.shape[1]), lambda step: (jnp.maximum(step - skipped, 0), 0))

    return spec


def row_parts(skipped, parts):
    def spec(array):
        return pl.BlockSpec(
            (array.shape[0] // parts, array.shape[1]), lambda step: (jnp.maximum(step - skipped, 0), 0)
        )

    return spec


def column_parts(skipped, parts):
    def spec(array):
        return pl.BlockSpec(
            (array.shape[0], array.shape[1] // parts), lambda step: (0, jnp.maximum(step - skipped, 0))
        )

    return spec


SCALAR = pl.BlockSpec(memory_space=pltpu.SMEM)


def shaped(dims, dtype):
    return jax.ShapeDtypeStruct(dims, dtype)


def call(kernel, steps, operands, results, scratch=(), flops=0, limit=56, after=()):
    arrays = [array for array, spec in operands]
    moved = sum(array.size * array.dtype.itemsize for array in arrays)
    moved += sum(array.size * array.dtype.itemsize for array, spec in results)
    if after:
        inner = kernel
        start, stop = len(operands), len(operands) + len(after)
        operands = operands + [(array, pl.BlockSpec(memory_space=pl.ANY)) for array in after]
        arrays = arrays + list(after)

        def kernel(*refs):
            inner(*refs[:start], *refs[stop:])

    return pl.pallas_call(
        kernel,
        grid=(steps,),
        in_specs=[spec if isinstance(spec, pl.BlockSpec) else spec(array) for array, spec in operands],
        out_specs=[spec if isinstance(spec, pl.BlockSpec) else spec(array) for array, spec in results],
        out_shape=[array for array, spec in results],
        scratch_shapes=list(scratch),
        compiler_params=pltpu.CompilerParams(vmem_limit_bytes=limit << 20),
        cost_estimate=pl.CostEstimate(flops=flops, bytes_accessed=moved, transcendentals=0),
    )(*arrays)


def bits_of(axis):
    return lax.axis_size(axis).bit_length() - 1


def exchange(values, axis, bit):
    count = lax.axis_size(axis)
    return lax.ppermute(values, axis, [(at, at ^ (1 << bit)) for at in range(count)])


def own_bit(axis, bit):
    return (lax.axis_index(axis) >> bit) & 1


def every_bit():
    return [(axis, bit) for axis in AXES for bit in range(bits_of(axis))]


def sending(values, axis, bit):
    half = values.shape[0] // 2
    return lax.dynamic_slice_in_dim(values, (1 - own_bit(axis, bit)) * half, half)


def keeping(values, axis, bit):
    half = values.shape[0] // 2
    return lax.dynamic_slice_in_dim(values, own_bit(axis, bit) * half, half)


def merged(values, arrived, axis, bit):
    upper = own_bit(axis, bit) == 1
    return jnp.concatenate([jnp.where(upper, arrived, values), jnp.where(upper, values, arrived)])


def part_orders():
    pair = every_bit()[0]
    rest_dp = [step for step in every_bit()[1:] if step[0] == "dp"]
    rest_stream = [step for step in every_bit() if step[0] == "stream"]
    return [
        [pair] + rest_dp + rest_stream,
        [pair] + rest_dp[::-1] + rest_stream[::-1],
        [pair] + rest_stream + rest_dp,
    ]


def reduce_kernel(slots, tops):
    count = len(slots)

    def kernel(bits, *refs):
        for at, (slot, top) in enumerate(zip(slots, tops)):
            kept, arrived = refs[2 * at], refs[2 * at + 1]
            rows = arrived.shape[0]
            base = 0 if top is None else pl.multiple_of(bits[top] * rows, 8)
            if slot is None:
                refs[2 * count + at][...] = kept[pl.ds(base, rows), :] + arrived[...]
                continue
            half = rows // 2
            for out, bit in ((2 * count + 2 * at, 1 - bits[slot]), (2 * count + 2 * at + 1, bits[slot])):
                start = pl.multiple_of(bit * half, 8)
                refs[out][...] = kept[pl.ds(base + start, half), :] + arrived[pl.ds(start, half), :]

    return kernel


def split_kernel(slots):
    def kernel(bits, *refs):
        count = len(slots)
        copies = []
        for at, slot in enumerate(slots):
            whole_part, half_part = refs[at], refs[count + at]
            rows = half_part.shape[0]
            start = pl.multiple_of((1 - bits[slot]) * rows, 8)
            copies.append(
                pltpu.make_async_copy(whole_part.at[pl.ds(start, rows), :], half_part, refs[2 * count].at[at])
            )
        for copy in copies:
            copy.start()
        for copy in copies:
            copy.wait()

    return kernel


def gather_kernel(slots):
    count = len(slots)

    def kernel(bits, *refs):
        for at, slot in enumerate(slots):
            mine, arrived, out = refs[2 * at], refs[2 * at + 1], refs[2 * count + at]
            rows = mine.shape[0]
            out[pl.ds(pl.multiple_of(bits[slot] * rows, 8), rows), :] = mine[...]
            out[pl.ds(pl.multiple_of((1 - bits[slot]) * rows, 8), rows), :] = arrived[...]

    return kernel


def one_block(array):
    return pl.BlockSpec(array.shape, lambda step: (0, 0))


class Group:
    def __init__(self, bits, parts, orders, split=False):
        self.bits = bits
        self.orders = [part_orders()[which] for which in orders]
        self.kept = parts
        if split:
            self.sends = call(
                split_kernel(self.slots(0)),
                1,
                [(bits, SCALAR)] + [(part, pl.BlockSpec(memory_space=pl.ANY)) for part in parts],
                [(shaped((part.shape[0] // 2, part.shape[1]), F32), one_block) for part in parts],
                scratch=[pltpu.SemaphoreType.DMA((len(parts),))],
                flops=STAGE_FLOPS,
                limit=STAGE_LIMIT,
            )
        else:
            self.sends = [sending(part, *order[0]) for part, order in zip(parts, self.orders)]
        self.steps = len(self.orders[0])

    def slots(self, at):
        return [every_bit().index(order[at]) for order in self.orders]

    def run(self, kernel, operands, results):
        return call(
            kernel,
            1,
            [(self.bits, SCALAR)] + [(array, one_block) for array in operands],
            [(shaped(dims, F32), one_block) for dims in results],
            flops=STAGE_FLOPS,
            limit=STAGE_LIMIT,
        )

    def reduce(self, at):
        arrived = [exchange(send, *order[at]) for send, order in zip(self.sends, self.orders)]
        tops = self.slots(0) if at == 0 else [None] * len(arrived)
        last = at == self.steps - 1
        slots = [None] * len(arrived) if last else self.slots(at + 1)
        pairs = [array for pair in zip(self.kept, arrived) for array in pair]
        if last:
            self.kept = self.run(reduce_kernel(slots, tops), pairs, [array.shape for array in arrived])
            return
        halves = [(array.shape[0] // 2, array.shape[1]) for array in arrived for twice in range(2)]
        if any(dims[0] % 8 for dims in halves):
            sums = [
                (kept if top is None else keeping(kept, *order[0])) + got
                for kept, got, top, order in zip(self.kept, arrived, tops, self.orders)
            ]
            self.sends = [sending(total, *order[at + 1]) for total, order in zip(sums, self.orders)]
            self.kept = [keeping(total, *order[at + 1]) for total, order in zip(sums, self.orders)]
            return
        found = self.run(reduce_kernel(slots, tops), pairs, halves)
        self.sends, self.kept = found[0::2], found[1::2]

    def gather(self, at):
        arrived = [exchange(mine, *order[at]) for mine, order in zip(self.kept, self.orders)]
        if any(array.shape[0] % 8 for array in arrived):
            self.kept = [
                merged(mine, got, *order[at]) for mine, got, order in zip(self.kept, arrived, self.orders)
            ]
            return
        pairs = [array for pair in zip(self.kept, arrived) for array in pair]
        doubled = [(2 * array.shape[0], array.shape[1]) for array in arrived]
        self.kept = self.run(gather_kernel(self.slots(at)), pairs, doubled)


def sum_groups(groups):
    steps = groups[0].steps
    for at in range(steps):
        for group in groups:
            group.reduce(at)
    for at in reversed(range(steps)):
        for group in groups:
            group.gather(at)
    return [group.kept for group in groups]


def sum_small(values):
    for axis, bit in every_bit():
        values = values + exchange(values, axis, bit)
    return values


def join_moments(packed):
    for axis, bit in every_bit():
        other = exchange(packed, axis, bit)
        both = packed + other
        gap = packed[1] / packed[0] - other[1] / other[0]
        extra = gap * gap * (packed[0] * other[0] / both[0])
        packed = jnp.concatenate([both[0:2], both[2:3] + extra[None], both[3:]])
    return packed


def body(
    inputs, lengths, cotangent,
    gain_one, shift_one, expand_one, lift_one, reduce_one, offset_one,
    attend_gain, attend_shift, query_proj, query_bias, key_proj, value_proj, value_bias, output_proj, output_bias,
    mixing_gain, mixing_shift, point_first, first_bias, depth_kernel, batch_gain, batch_shift, point_second, second_bias,
    gain_two, shift_two, expand_two, lift_two, reduce_two, offset_two, final_gain, final_shift,
):
    utterances, frames, width = inputs.shape
    hidden = expand_one.shape[1]
    steps = frames // TILE
    x = inputs.reshape(frames, width)
    cotangent_rows = cotangent.reshape(frames, width)
    vectors = [
        gain_one, shift_one, offset_one, attend_gain, attend_shift, query_bias, value_bias, output_bias,
        mixing_gain, mixing_shift, batch_gain, batch_shift, second_bias, gain_two, shift_two, offset_two,
        final_gain, final_shift, first_bias, depth_kernel, lift_one, lift_two,
    ]
    table, lift_first, lift_second = call(
        table_kernel,
        1,
        [(vector, whole) for vector in vectors],
        [(shaped(dims, F32), whole) for dims in ((32, width), (1, hidden), (1, hidden))],
        limit=60,
    )
    rows_low = shaped((frames, width), LOW)
    rows_full = shaped((frames, width), F32)
    hidden_low = shaped((frames, hidden), LOW)
    heads_low = shaped((HEADS, frames, LANES), LOW)

    def small(rows):
        return (shaped((rows, width), F32), whole)

    behind = late(steps)
    (
        normed_a, acted_a, slope_a, x1, normed_b, keys, values,
        again, mixed_wide, mixed, x2, normed_c, gated, gate_c, convolved, moments, sums_a,
    ) = call(
        forward_kernel,
        2 * steps,
        [
            (lengths, SCALAR), (x, early), (table, whole), (lift_first, whole), (expand_one, whole),
            (reduce_one, whole), (query_proj, whole), (key_proj, whole), (value_proj, whole),
            (output_proj, whole), (point_first, whole),
        ],
        [
            (rows_low, early), (hidden_low, early), (hidden_low, early), (rows_full, early), (rows_low, early),
            (heads_low, early), (heads_low, early),
            (heads_low, behind), (rows_full, behind), (rows_low, behind), (rows_full, behind), (rows_low, behind),
            (rows_full, behind), (rows_full, behind), (rows_full, whole), small(8), small(8),
        ],
        scratch=[
            pltpu.VMEM((HEADS, frames, LANES), LOW),
            pltpu.VMEM((HEADS, frames, LANES), LOW),
            pltpu.VMEM((HEADS, frames, LANES), LOW),
            pltpu.VMEM((frames, width), F32),
            pltpu.VMEM((frames + 16, width), F32),
        ],
        limit=56,
        flops=2 * frames * width * (2 * hidden + 3 * width) + 8 * frames * frames * width,
    )
    moments = join_moments(moments)
    (
        block_output, g3, direct, grad_reduce_two, grad_expand_two, grad_second, sums_c, lift_two_sums,
    ) = call(
        rear_kernel,
        steps + 4,
        [
            (lengths, SCALAR), (convolved, early), (x2, early), (cotangent_rows, early), (moments, whole),
            (table, whole), (lift_second, whole), (point_second, whole), (expand_two, whole), (reduce_two, whole),
        ],
        [
            (rows_low, early), (rows_full, early), (rows_full, early),
            (shaped((hidden, width), F32), row_parts(steps, 4)), (shaped((width, hidden), F32), row_parts(steps, 4)),
            (shaped((width, width), F32), row_parts(steps, 4)), small(16), small(8),
        ],
        scratch=[
            pltpu.VMEM((frames, width), LOW),
            pltpu.VMEM((frames, width), LOW),
            pltpu.VMEM((frames, hidden), LOW),
            pltpu.VMEM((frames, width), LOW),
            pltpu.VMEM((frames, width), LOW),
            pltpu.VMEM((frames, hidden), LOW),
        ],
        limit=56,
        flops=2 * frames * width * (6 * hidden + 3 * width),
    )
    batch_sums = sum_small(sums_c[0:8])
    second_large = lax.psum((grad_expand_two, grad_reduce_two), AXES)
    g2, mixed_grads, grad_point_first, grad_output, sums_d = call(
        mixing_kernel,
        2 * steps + 2,
        [
            (lengths, SCALAR), (moments, whole), (batch_sums, whole), (direct, whole), (convolved, whole),
            (gated, early_half), (gate_c, early_half), (x2, early_half), (g3, early_half), (mixed_wide, early_half), (table, whole),
            (point_first, whole), (output_proj, whole), (normed_c, column_parts(2 * steps, 2)), (mixed, column_parts(2 * steps, 2)),
        ],
        [
            (rows_full, early_half), (heads_low, early_half), (shaped((width, 2 * width), F32), row_parts(2 * steps, 2)),
            (shaped((width, width), F32), row_parts(2 * steps, 2)), small(16),
        ],
        scratch=[
            pltpu.VMEM((frames + 16, width), F32),
            pltpu.VMEM((frames, 2 * width), LOW),
            pltpu.VMEM((frames, width), LOW),
        ],
        limit=56,
        flops=2 * frames * width * 6 * width,
    )
    pair_block = pl.BlockSpec((2, frames, LANES), lambda step: (step, 0, 0))
    lane_block = pl.BlockSpec((frames, LANES), lambda step: (0, step))
    query_grad, key_grad, value_grad = call(
        attend_back_kernel,
        HEADS // 2,
        [(again, pair_block), (keys, pair_block), (values, pair_block), (mixed_grads, pair_block)],
        [(rows_low, lane_block), (rows_low, lane_block), (rows_low, lane_block)],
        limit=20,
        flops=20 * frames * frames * width,
    )
    parts = row_parts(steps, 4)
    (
        input_gradient, grad_reduce_one, grad_expand_one, grad_query, grad_key, grad_value, sums_e, lift_one_sums,
    ) = call(
        first_back_kernel,
        steps + 4,
        [
            (query_grad, whole), (key_grad, whole), (value_grad, whole), (x1, early), (g2, early), (slope_a, early),
            (table, whole), (query_proj, whole), (key_proj, whole), (value_proj, whole), (reduce_one, whole),
            (acted_a, column_parts(steps, 4)), (normed_a, column_parts(steps, 4)), (normed_b, column_parts(steps, 4)),
            (x, early), (expand_one, whole),
        ],
        [
            (rows_low, early), (shaped((hidden, width), F32), parts),
            (shaped((width, hidden), F32), parts), (shaped((width, width), F32), parts),
            (shaped((width, width), F32), parts), (shaped((width, width), F32), parts), small(8), small(8),
        ],
        scratch=[pltpu.VMEM((frames, width), LOW), pltpu.VMEM((frames, hidden), LOW)],
        limit=44,
        flops=2 * frames * width * (3 * hidden + 6 * width),
    )
    bits = jnp.stack([own_bit(axis, bit) for axis, bit in every_bit()]).astype(jnp.int32)
    small_rows = jnp.concatenate(
        [sums_a, sums_c, lift_two_sums, sums_d, sums_e, lift_one_sums, jnp.zeros((192, width), F32)]
    )
    groups = [
        Group(bits, [grad_reduce_one, grad_expand_one], (0, 1), split=True),
        Group(
            bits,
            [
                grad_point_first,
                jnp.concatenate([grad_second, grad_output]),
                jnp.concatenate([grad_query, grad_key, grad_value, small_rows]),
            ],
            (0, 1, 2),
        ),
    ]
    (first_reduce, first_expand), (sum_point_first, sum_square, third) = sum_groups(groups)
    tail = third[3 * width :]
    total_a, total_c, total_lift, total_d, total_e, total_lift_one = (
        tail[0:8], tail[8:24], tail[24:32], tail[32:48], tail[48:56], tail[56:64],
    )
    squares = jnp.sum(
        jnp.stack(
            [
                total_a[0], total_a[2], total_c[8], total_c[10], total_a[1], total_a[3], total_c[9], total_c[11],
            ]
        ),
        axis=1,
    )
    rms_stats = jnp.sqrt(squares / (moments[0, 0] * width))

    return (
        block_output.reshape(inputs.shape),
        input_gradient.reshape(inputs.shape),
        total_e[5],
        total_e[6],
        first_expand,
        total_lift_one[0 : hidden // width].reshape(-1),
        first_reduce,
        total_e[4],
        total_e[0],
        total_e[1],
        third[:width],
        total_e[2],
        third[width : 2 * width],
        third[2 * width : 3 * width],
        total_e[3],
        sum_square[width:],
        total_d[13],
        total_d[0],
        total_d[1],
        sum_point_first,
        total_d[2:4].reshape(-1),
        total_d[4:13],
        batch_sums[1],
        batch_sums[0],
        sum_square[:width],
        total_c[2],
        total_c[3],
        total_c[4],
        second_large[0],
        total_lift[0 : hidden // width].reshape(-1),
        second_large[1],
        total_c[5],
        total_c[6],
        total_c[7],
        rms_stats,
    )


def solution(mesh):
    rows = P(AXES, None, None)
    return jax.shard_map(
        body,
        mesh=mesh,
        in_specs=(rows, P(AXES), rows) + (P(),) * 32,
        out_specs=(rows, rows) + (P(),) * 33,
        check_vma=False,
    )
```
